32 devices in a mesh: pairs: 8 (over z, x), sect: 4 (over y, core).
Axes of the slice: x: 2, y: 2, z: 4, core: 2. Of those that a mesh axis runs over, the one named last changes fastest.
Arguments:
- wavefunction: bfloat16 [4096, 1024], P('sect'), may hold values from -6 to 6
- left_normal: bfloat16 [16, 8, 512, 512], P('pairs', 'sect'), may hold values from -0.0625 to 0.0625
- left_comp: bfloat16 [16, 8, 512, 512], P('pairs', 'sect'), may hold values from -0.0625 to 0.0625
- right_comp: bfloat16 [16, 2, 512, 512], P('pairs'), may hold values from -0.25 to 0.25
- right_normal: bfloat16 [16, 2, 512, 512], P('pairs'), may hold values from -0.25 to 0.25
- pair_shift: int32 [16], P('pairs'), may hold values from 0 to 1
- pair_count: int32 [8], P('pairs'), may hold values from 1 to 2, as said below
- sector_rows: int32 [8], P('sect'), may hold values from 128 to 512, as said below
Outputs:
- sigma: bfloat16 [4096, 1024], P(('sect', 'pairs'))
The draws below stay inside these ranges and needn't reach their ends.
Inputs may be any that keep to these rules, and one draw needn't show every extreme that they name: Index i of pairs holds pair slots i * 2 to (i + 1) * 2 - 1, of which the first pair_count[i] are live; some index has all 2 live. Rows of sector s at or beyond sector_rows[s] are padding; some sector uses all 512 rows.
All inputs are finite; a program needn't handle non-finite values.
Results may differ from the reference program's by a relative error of at most 0.005.
Values may be sent and summed in bfloat16 or wider, within the bound.
A program may use at most 128 MiB of HBM per device.

```python
import jax
import jax.numpy as jnp
from jax import lax

B = 512
KB = 512
KS = 2
PAIR_DEV = 2
SECTORS = 8
PAIRS = 16
K = 1024
N_PAIRS = 8


def draw_pair_count(key, part):
    key_counts, key_chosen = jax.random.split(key)
    counts = jax.random.randint(key_counts, (N_PAIRS,), 1, PAIR_DEV + 1)
    chosen_index = jax.random.randint(key_chosen, (), 0, N_PAIRS)
    return jnp.where(jnp.arange(N_PAIRS) == chosen_index, PAIR_DEV, counts).astype(jnp.int32)


def draw_sector_rows(key, part):
    key_rows, key_chosen = jax.random.split(key)
    counts = jax.random.randint(key_rows, (SECTORS,), B // 4, B + 1)
    chosen_index = jax.random.randint(key_chosen, (), 0, SECTORS)
    return jnp.where(jnp.arange(SECTORS) == chosen_index, B, counts).astype(jnp.int32)


def set_ends(values, rng, low, top_value):
    longest = values.shape.index(max(values.shape))
    spots = []
    for shift in (0, 1):
        where = [jax.random.randint(jax.random.fold_in(rng, axis), (), 0, length) for axis, length in enumerate(values.shape)]
        where[longest] = (where[longest] + shift) % values.shape[longest]
        spots.append(tuple(where))
    return values.at[spots[0]].set(low).at[spots[1]].set(top_value)


def block_levels(stream_key, dims, cuts, smallest, high):
    gain, own = 1.0, jax.random.fold_in(stream_key, 6)
    for dim, blocks in cuts:
        draws = jnp.exp(jax.random.uniform(jax.random.fold_in(own, dim), (blocks,), jnp.float32, smallest / len(cuts), high / len(cuts)))
        gain = gain * jnp.repeat(draws, dims[dim] // blocks).reshape([-1 if axis == dim else 1 for axis in range(len(dims))])
    return gain


def centred(stream_key, dims, width, bound, shards=(), held_as=jnp.bfloat16):
    values = width * jax.random.normal(stream_key, dims, jnp.float32)
    if shards:
        values = values * block_levels(stream_key, dims, shards, -0.22, 0.18)
    return jnp.clip(values, -bound, bound).astype(held_as)


def setup_inputs(seed: int = 0) -> dict:
    key_list = jax.random.split(jax.random.key(seed), 9)
    return {
        "wavefunction": centred(key_list[0], (SECTORS * B, K), 1.0, 6.0, ((0, 4),)),
        "left_normal": centred(key_list[1], (PAIRS, SECTORS, B, B), (B * PAIRS) ** -0.5, 0.0625, ((0, 8), (1, 4))),
        "left_comp": centred(key_list[2], (PAIRS, SECTORS, B, B), (B * PAIRS) ** -0.5, 0.0625, ((0, 8), (1, 4))),
        "right_comp": centred(key_list[3], (PAIRS, KS, KB, KB), KB ** -0.5, 0.25, ((0, 8),)),
        "right_normal": centred(key_list[4], (PAIRS, KS, KB, KB), KB ** -0.5, 0.25, ((0, 8),)),
        "pair_shift": set_ends(jax.random.randint(key_list[5], (PAIRS,), 0, KS), jax.random.fold_in(key_list[5], 1), 0, KS - 1).astype(jnp.int32),
        "pair_count": draw_pair_count(jax.random.fold_in(key_list[8], 71), 0),
        "sector_rows": draw_sector_rows(jax.random.fold_in(key_list[8], 71), 0),
    }


def reference(wavefunction, left_normal, left_comp, right_comp, right_normal, pair_shift, pair_count, sector_rows):
    row_ids = jnp.arange(B, dtype=jnp.int32)
    row_keep = row_ids[None, :] < sector_rows[:, None]
    blocked = wavefunction.reshape(SECTORS, B, K)
    masked = jnp.where(row_keep[:, :, None], blocked, jnp.zeros((), jnp.bfloat16))
    earlier = jnp.concatenate([jnp.zeros((1, B, K), jnp.bfloat16), masked[:-1]], axis=0)
    masked_wide = masked.astype(jnp.float32)
    earlier_wide = earlier.astype(jnp.float32)
    slot_ids = jnp.arange(PAIRS, dtype=jnp.int32)
    live = (slot_ids % PAIR_DEV) < pair_count[slot_ids // PAIR_DEV]

    def right_apply(left_part, offset, right_ops):
        rolled = jnp.roll(left_part.reshape(SECTORS, B, KS, KB), -offset, axis=2)
        return jnp.einsum('sikb,kcb->sikc', rolled.astype(jnp.float32), right_ops.astype(jnp.float32))

    def one_pair(totals, pieces):
        normal_op, comp_op, rcomp_op, rnormal_op, offset, active = pieces

        def accumulate(current):
            normal_left = jnp.einsum('sij,sjk->sik', normal_op.astype(jnp.float32), masked_wide).astype(jnp.bfloat16)
            comp_left = jnp.einsum('sij,sjk->sik', comp_op.astype(jnp.float32), earlier_wide).astype(jnp.bfloat16)
            return current + right_apply(normal_left, offset, rcomp_op) + right_apply(comp_left, offset, rnormal_op)

        return lax.cond(active, accumulate, lambda current: current, totals), None

    start = jnp.zeros((SECTORS, B, KS, KB), jnp.float32)
    totals, _ = lax.scan(one_pair, start, (left_normal, left_comp, right_comp, right_normal, pair_shift, live))
    totals = totals.reshape(SECTORS, B, K)
    result = jnp.where(row_keep[:, :, None], totals, jnp.zeros((), jnp.float32))
    return result.reshape(SECTORS * B, K).astype(jnp.bfloat16)
```

```python
import functools

import jax
import jax.numpy as jnp
from jax import lax
from jax.experimental import pallas as pl
from jax.experimental.pallas import tpu as pltpu
from jax.sharding import PartitionSpec as P

MESH = pl.DeviceIdType.MESH
F32 = jnp.float32
BF16 = jnp.bfloat16
NT = (((1,), (1,)), ((), ()))


def x_size(count):
    return 1 << ((count.bit_length() - 1) // 2)


def kernel(
    nz,
    nx,
    ns,
    shift_ref,
    count_ref,
    rows_ref,
    wave,
    left_normal,
    left_comp,
    right_comp,
    right_normal,
    out_ref,
    waves,
    lefts,
    rights,
    applied,
    total,
    own,
    x_out,
    x_in,
    z_out,
    z_in,
    far_in,
    load_sem,
    halo_send,
    halo_recv,
    x_send,
    x_recv,
    z_send,
    z_recv,
    far_recv,
):
    pair_dev, sec_dev, width, _ = left_normal.shape
    blocks, cols = right_comp.shape[1], right_comp.shape[2]
    chunk = sec_dev * width // nz
    part = chunk // nx
    me = lax.axis_index("pairs")
    sect = lax.axis_index("sect")
    z = me // nx
    x = lax.rem(me, nx)
    partner = z + 1 - 2 * lax.rem(z, 2)

    loads = {}

    def load(name, source, target):
        copy = pltpu.make_async_copy(source, target, load_sem.at[len(loads)])
        copy.start()
        loads[name] = copy

    for s in reversed(range(sec_dev)):
        load(("wave", s), wave.at[pl.ds(s * width, width)], waves.at[s + 1])
    for s in reversed(range(sec_dev)):
        for p in range(pair_dev):
            load(("normal", s, p), left_normal.at[p, s], lefts.at[0, p, s])
            load(("comp", s, p), left_comp.at[p, s], lefts.at[1, p, s])
        if s == sec_dev - 1:
            load("right_comp", right_comp, rights.at[0])
            load("right_normal", right_normal, rights.at[1])

    barrier = pltpu.get_barrier_semaphore()
    for d in range(1, nx):
        pl.semaphore_signal(barrier, inc=1, device_id=(z * nx + lax.rem(x + d, nx), sect), device_id_type=MESH)
    for d in range(1, nz):
        pl.semaphore_signal(barrier, inc=1, device_id=(lax.rem(z + d, nz) * nx + x, sect), device_id_type=MESH)
    for d in (1, ns - 1):
        pl.semaphore_signal(barrier, inc=1, device_id=(me, lax.rem(sect + d, ns)), device_id_type=MESH)

    def mask(s):
        loads[("wave", s)].wait()
        step = 64

        def body(i, _):
            at = pl.ds(i * step, step)
            keep = lax.broadcasted_iota(jnp.int32, (step, blocks * cols), 0) + i * step < rows_ref[s]
            value = waves[s + 1, at, :].astype(F32)
            waves[s + 1, at, :] = jnp.where(keep, value, 0.0).astype(BF16)
            return 0

        lax.fori_loop(0, width // step, body, 0)

    mask(sec_dev - 1)
    pl.semaphore_wait(barrier, nx - 1 + nz - 1 + 2)
    halo = pltpu.make_async_remote_copy(
        src_ref=waves.at[sec_dev],
        dst_ref=waves.at[0],
        send_sem=halo_send,
        recv_sem=halo_recv,
        device_id=(me, lax.rem(sect + 1, ns)),
        device_id_type=MESH,
    )

    @pl.when(sect < ns - 1)
    def _():
        halo.start()

    @pl.when(sect == 0)
    def _():
        waves[0] = jnp.zeros((width, blocks * cols), BF16)

    for s in reversed(range(sec_dev - 1)):
        mask(s)

    def order(k):
        down = nz - 1 - k
        return jnp.where(k == nz - 1, z, jnp.where(down > z, down, down - 1))

    def x_copy(c, d, j):
        return pltpu.make_async_remote_copy(
            src_ref=x_out.at[c, d - 1, j],
            dst_ref=x_in.at[c, d - 1, j],
            send_sem=x_send.at[c, d - 1, j],
            recv_sem=x_recv.at[c, d - 1, j],
            device_id=(z * nx + lax.rem(x + d, nx), sect),
            device_id_type=MESH,
        )

    def z_copy(c, j):
        return pltpu.make_async_remote_copy(
            src_ref=z_out.at[c, j],
            dst_ref=z_in.at[c, j],
            send_sem=z_send.at[c, j],
            recv_sem=z_recv.at[c, j],
            device_id=(partner * nx + x, sect),
            device_id_type=MESH,
        )

    def far_copy(c, j, slot):
        return pltpu.make_async_remote_copy(
            src_ref=z_out.at[c, j],
            dst_ref=far_in.at[slot, j],
            send_sem=z_send.at[c, j],
            recv_sem=far_recv.at[slot, j],
            device_id=(c * nx + x, sect),
            device_id_type=MESH,
        )

    def combines(c):
        above = (c // 2 > z // 2) & (lax.rem(z, 2) == 1)
        below = (c // 2 < z // 2) & (lax.rem(z, 2) == 0)
        return above | below

    def compute(k):
        c = order(k)
        s = c * chunk // width
        at = pl.ds(pl.multiple_of(c * chunk - s * width, chunk), chunk)
        for p in range(pair_dev):
            live = p < count_ref[0]
            offset = shift_ref[p]
            for kind in range(2):
                ops = lefts[kind, p, s, at, :]
                value = jnp.dot(ops, waves[s + 1 - kind], preferred_element_type=F32)
                value = jnp.where(live, value, 0.0).astype(BF16)
                pieces = [value[:, j * cols : (j + 1) * cols] for j in range(blocks)]
                for j in range(blocks):
                    piece = pieces[j]
                    for o in range(1, blocks):
                        piece = jnp.where(offset == o, pieces[(j + o) % blocks], piece)
                    applied[j, kind, p] = piece
        for j in range(blocks):
            result = None
            for kind in range(2):
                for p in range(pair_dev):
                    term = lax.dot_general(applied[j, kind, p], rights[kind, p, j], NT, preferred_element_type=F32)
                    result = term if result is None else result + term
            total[...] = result
            own[c, j] = total[pl.ds(pl.multiple_of(x * part, part), part), :]
            for d in range(1, nx):
                to = lax.rem(x + d, nx)
                x_out[c, d - 1, j] = total[pl.ds(pl.multiple_of(to * part, part), part), :].astype(BF16)
                x_copy(c, d, j).start()

    def x_sum(k):
        c = order(k)
        for j in range(blocks):
            value = own[c, j]
            for d in range(1, nx):
                x_copy(c, d, j).wait_recv()
                value = value + x_in[c, d - 1, j].astype(F32)
            own[c, j] = value

            @pl.when((c != z) & jnp.logical_not(combines(c)))
            def _():
                z_out[c, j] = value.astype(BF16)
                z_copy(c, j).start()

    def z_sum(k):
        c = order(k)

        @pl.when((c != z) & combines(c))
        def _():
            for j in range(blocks):
                z_copy(c, j).wait_recv()
                z_out[c, j] = (own[c, j] + z_in[c, j].astype(F32)).astype(BF16)
                far_copy(c, j, z // 2).start()

    last = sec_dev - 1
    for p in range(pair_dev):
        loads[("normal", last, p)].wait()
        loads[("comp", last, p)].wait()
    loads["right_comp"].wait()
    loads["right_normal"].wait()
    for s in range(last):
        for p in range(pair_dev):
            loads[("normal", s, p)].wait()
            loads[("comp", s, p)].wait()

    halo_step = nz - nz // sec_dev - jnp.where(z >= nz // sec_dev, 1, 0)

    def step(k, _):
        @pl.when((k == halo_step) & (sect > 0))
        def _():
            halo.wait_recv()

        @pl.when(k < nz)
        def _():
            compute(k)

        @pl.when((k >= 1) & (k <= nz))
        def _():
            x_sum(k - 1)

        @pl.when(k >= 2)
        def _():
            z_sum(k - 2)

        return 0

    lax.fori_loop(0, nz + 1, step, 0)

    for j in range(blocks):
        value = own[z, j]
        z_copy(z, j).wait_recv()
        value = value + z_in[z, j].astype(F32)
        for d in range(1, nz // 2):
            slot = lax.rem(z // 2 + d, nz // 2)
            far_copy(z, j, slot).wait_recv()
            value = value + far_in[slot, j].astype(F32)
        out_ref[:, j * cols : (j + 1) * cols] = value.astype(BF16)

    @pl.when(sect < ns - 1)
    def _():
        halo.wait_send()

    def drain(k, _):
        c = order(k)
        for j in range(blocks):
            for d in range(1, nx):
                x_copy(c, d, j).wait_send()

            @pl.when(c != z)
            def _():
                z_copy(c, j).wait_send()

        return 0

    lax.fori_loop(0, nz, drain, 0)


def solution(mesh):
    n_pairs, ns = mesh.shape["pairs"], mesh.shape["sect"]
    nx = x_size(n_pairs)
    nz = n_pairs // nx

    def local(wavefunction, left_normal, left_comp, right_comp, right_normal, pair_shift, pair_count, sector_rows):
        pair_dev, sec_dev, width, _ = left_normal.shape
        blocks, cols = right_comp.shape[1], right_comp.shape[2]
        chunk = sec_dev * width // nz
        part = chunk // nx
        dma = pltpu.SemaphoreType.DMA
        smem = pl.BlockSpec(memory_space=pltpu.SMEM)
        hbm = pl.BlockSpec(memory_space=pl.ANY)
        summed = pl.pallas_call(
            functools.partial(kernel, nz, nx, ns),
            out_shape=jax.ShapeDtypeStruct((part, blocks * cols), BF16),
            in_specs=[smem] * 3 + [hbm] * 5,
            out_specs=pl.BlockSpec(memory_space=pltpu.VMEM),
            scratch_shapes=[
                pltpu.VMEM((sec_dev + 1, width, blocks * cols), BF16),
                pltpu.VMEM((2, pair_dev, sec_dev, width, width), BF16),
                pltpu.VMEM((2, pair_dev, blocks, cols, cols), BF16),
                pltpu.VMEM((blocks, 2, pair_dev, chunk, cols), BF16),
                pltpu.VMEM((chunk, cols), F32),
                pltpu.VMEM((nz, blocks, part, cols), F32),
                pltpu.VMEM((nz, nx - 1, blocks, part, cols), BF16),
                pltpu.VMEM((nz, nx - 1, blocks, part, cols), BF16),
                pltpu.VMEM((nz, blocks, part, cols), BF16),
                pltpu.VMEM((nz, blocks, part, cols), BF16),
                pltpu.VMEM((nz // 2, blocks, part, cols), BF16),
                dma((sec_dev + 2 * sec_dev * pair_dev + 2,)),
                dma,
                dma,
                dma((nz, nx - 1, blocks)),
                dma((nz, nx - 1, blocks)),
                dma((nz, blocks)),
                dma((nz, blocks)),
                dma((nz // 2, blocks)),
            ],
            compiler_params=pltpu.CompilerParams(
                collective_id=0, has_side_effects=True, vmem_limit_bytes=48 * 2**20
            ),
        )(pair_shift, pair_count, sector_rows, wavefunction, left_normal, left_comp, right_comp, right_normal)
        first = lax.axis_index("pairs") * part
        kept = sector_rows[first // width]
        row = lax.broadcasted_iota(jnp.int32, (part, blocks * cols), 0) + lax.rem(first, width)
        return jnp.where(row < kept, summed, jnp.zeros((), BF16))

    placed = (
        P("sect", None),
        P("pairs", "sect", None, None),
        P("pairs", "sect", None, None),
        P("pairs", None, None, None),
        P("pairs", None, None, None),
        P("pairs"),
        P("pairs"),
        P("sect"),
    )
    return jax.shard_map(
        local, mesh=mesh, in_specs=placed, out_specs=P(("sect", "pairs"), None), check_vma=False
    )
```

```python
import functools

import jax
import jax.numpy as jnp
from jax import lax
from jax.experimental import pallas as pl
from jax.experimental.pallas import tpu as pltpu
from jax.sharding import PartitionSpec as P

MESH = pl.DeviceIdType.MESH
F32 = jnp.float32
BF16 = jnp.bfloat16
NT = (((1,), (1,)), ((), ()))


def x_size(count):
    return 1 << ((count.bit_length() - 1) // 2)


def kernel(
    nz,
    nx,
    ns,
    shift_ref,
    count_ref,
    rows_ref,
    wave,
    left_normal,
    left_comp,
    right_comp,
    right_normal,
    out_ref,
    waves,
    lefts,
    rights,
    applied,
    total,
    own,
    x_out,
    x_in,
    z_out,
    z_in,
    far_in,
    load_sem,
    halo_send,
    halo_recv,
    x_send,
    x_recv,
    z_send,
    z_recv,
    far_recv,
):
    pair_dev, sec_dev, width, _ = left_normal.shape
    blocks, cols = right_comp.shape[1], right_comp.shape[2]
    chunk = sec_dev * width // nz
    part = chunk // nx
    me = lax.axis_index("pairs")
    sect = lax.axis_index("sect")
    z = me // nx
    x = lax.rem(me, nx)
    partner = z + 1 - 2 * lax.rem(z, 2)

    late = (sect > 0) & (lax.rem(sect, 2) == 0)
    mirrored = (z >= nz // 2) & jnp.logical_not(late)

    loads = {}

    def load(name, source, target):
        copy = pltpu.make_async_copy(source, target, load_sem.at[len(loads)])
        copy.start()
        loads[name] = copy

    for s in reversed(range(sec_dev)):
        load(("wave", s), wave.at[pl.ds(s * width, width)], waves.at[s + 1])
    for i in range(sec_dev):
        s = jnp.where(mirrored, i, sec_dev - 1 - i)
        for p in range(pair_dev):
            load(("normal", i, p), left_normal.at[p, s], lefts.at[0, p, s])
            load(("comp", i, p), left_comp.at[p, s], lefts.at[1, p, s])
        if i == 0:
            load("right_comp", right_comp, rights.at[0])
            load("right_normal", right_normal, rights.at[1])

    barrier = pltpu.get_barrier_semaphore()
    for d in range(1, nx):
        pl.semaphore_signal(barrier, inc=1, device_id=(z * nx + lax.rem(x + d, nx), sect), device_id_type=MESH)
    for d in range(1, nz):
        pl.semaphore_signal(barrier, inc=1, device_id=(lax.rem(z + d, nz) * nx + x, sect), device_id_type=MESH)
    for d in (1, ns - 1):
        pl.semaphore_signal(barrier, inc=1, device_id=(me, lax.rem(sect + d, ns)), device_id_type=MESH)

    def mask(s):
        loads[("wave", s)].wait()
        step = 64

        def body(i, _):
            at = pl.ds(i * step, step)
            keep = lax.broadcasted_iota(jnp.int32, (step, blocks * cols), 0) + i * step < rows_ref[s]
            value = waves[s + 1, at, :].astype(F32)
            waves[s + 1, at, :] = jnp.where(keep, value, 0.0).astype(BF16)
            return 0

        lax.fori_loop(0, width // step, body, 0)

    mask(sec_dev - 1)
    pl.semaphore_wait(barrier, nx - 1 + nz - 1 + 2)
    halo = pltpu.make_async_remote_copy(
        src_ref=waves.at[sec_dev],
        dst_ref=waves.at[0],
        send_sem=halo_send,
        recv_sem=halo_recv,
        device_id=(me, lax.rem(sect + 1, ns)),
        device_id_type=MESH,
    )

    @pl.when(sect < ns - 1)
    def _():
        halo.start()

    @pl.when(sect == 0)
    def _():
        waves[0] = jnp.zeros((width, blocks * cols), BF16)

    for s in reversed(range(sec_dev - 1)):
        mask(s)

    def order(k):
        down = nz - 1 - k
        at = jnp.where(mirrored, nz - 1 - z, z)
        c = jnp.where(k == nz - 1, at, jnp.where(down > at, down, down - 1))
        return jnp.where(mirrored, nz - 1 - c, c)

    def x_copy(c, d, j):
        return pltpu.make_async_remote_copy(
            src_ref=x_out.at[c, d - 1, j],
            dst_ref=x_in.at[c, d - 1, j],
            send_sem=x_send.at[c, d - 1, j],
            recv_sem=x_recv.at[c, d - 1, j],
            device_id=(z * nx + lax.rem(x + d, nx), sect),
            device_id_type=MESH,
        )

    def z_copy(c, j):
        return pltpu.make_async_remote_copy(
            src_ref=z_out.at[c, j],
            dst_ref=z_in.at[c, j],
            send_sem=z_send.at[c, j],
            recv_sem=z_recv.at[c, j],
            device_id=(partner * nx + x, sect),
            device_id_type=MESH,
        )

    def far_copy(c, j, slot):
        return pltpu.make_async_remote_copy(
            src_ref=z_out.at[c, j],
            dst_ref=far_in.at[slot, j],
            send_sem=z_send.at[c, j],
            recv_sem=far_recv.at[slot, j],
            device_id=(c * nx + x, sect),
            device_id_type=MESH,
        )

    def combines(c):
        above = (c // 2 > z // 2) & (lax.rem(z, 2) == 1)
        below = (c // 2 < z // 2) & (lax.rem(z, 2) == 0)
        return above | below

    def compute(k):
        c = order(k)
        s = c * chunk // width
        at = pl.ds(pl.multiple_of(c * chunk - s * width, chunk), chunk)
        for p in range(pair_dev):
            live = p < count_ref[0]
            offset = shift_ref[p]
            for kind in range(2):
                ops = lefts[kind, p, s, at, :]
                value = jnp.dot(ops, waves[s + 1 - kind], preferred_element_type=F32)
                value = jnp.where(live, value, 0.0).astype(BF16)
                pieces = [value[:, j * cols : (j + 1) * cols] for j in range(blocks)]
                for j in range(blocks):
                    piece = pieces[j]
                    for o in range(1, blocks):
                        piece = jnp.where(offset == o, pieces[(j + o) % blocks], piece)
                    applied[j, kind, p] = piece

        @pl.when(k == 0)
        def _():
            loads["right_comp"].wait()
            loads["right_normal"].wait()

        for j in range(blocks):
            result = None
            for kind in range(2):
                for p in range(pair_dev):
                    term = lax.dot_general(applied[j, kind, p], rights[kind, p, j], NT, preferred_element_type=F32)
                    result = term if result is None else result + term
            total[...] = result
            own[c, j] = total[pl.ds(pl.multiple_of(x * part, part), part), :]
            for d in range(1, nx):
                to = lax.rem(x + d, nx)
                x_out[c, d - 1, j] = total[pl.ds(pl.multiple_of(to * part, part), part), :].astype(BF16)
                x_copy(c, d, j).start()

    def x_sum(k):
        c = order(k)
        for j in range(blocks):
            value = own[c, j]
            for d in range(1, nx):
                x_copy(c, d, j).wait_recv()
                value = value + x_in[c, d - 1, j].astype(F32)
            own[c, j] = value

            @pl.when((c != z) & jnp.logical_not(combines(c)))
            def _():
                z_out[c, j] = value.astype(BF16)
                z_copy(c, j).start()

    def z_sum(k):
        c = order(k)

        @pl.when((c != z) & combines(c))
        def _():
            for j in range(blocks):
                z_copy(c, j).wait_recv()
                z_out[c, j] = (own[c, j] + z_in[c, j].astype(F32)).astype(BF16)
                far_copy(c, j, z // 2).start()

    def wait_left(i):
        for p in range(pair_dev):
            loads[("normal", i, p)].wait()
            loads[("comp", i, p)].wait()

    wait_left(0)
    own_late = jnp.where(z >= nz // sec_dev, 1, 0)
    halo_step = jnp.where(mirrored, 0, nz - nz // sec_dev - own_late)

    def step(k, _):
        @pl.when(k == nz // sec_dev - 1)
        def _():
            for i in range(1, sec_dev):
                wait_left(i)

        @pl.when((k == halo_step) & (sect > 0))
        def _():
            halo.wait_recv()

        @pl.when(k < nz)
        def _():
            compute(k)

        @pl.when((k >= 1) & (k <= nz))
        def _():
            x_sum(k - 1)

        @pl.when(k >= 2)
        def _():
            z_sum(k - 2)

        return 0

    lax.fori_loop(0, nz + 1, step, 0)

    first = me * part
    row = lax.broadcasted_iota(jnp.int32, (part, cols), 0) + lax.rem(first, width)
    kept = row < rows_ref[first // width]
    for j in range(blocks):
        value = own[z, j]
        z_copy(z, j).wait_recv()
        value = value + z_in[z, j].astype(F32)
        for d in range(1, nz // 2):
            slot = lax.rem(z // 2 + d, nz // 2)
            far_copy(z, j, slot).wait_recv()
            value = value + far_in[slot, j].astype(F32)
        out_ref[:, j * cols : (j + 1) * cols] = jnp.where(kept, value, 0.0).astype(BF16)

    @pl.when(sect < ns - 1)
    def _():
        halo.wait_send()

    def drain(k, _):
        c = order(k)
        for j in range(blocks):
            for d in range(1, nx):
                x_copy(c, d, j).wait_send()

            @pl.when(c != z)
            def _():
                z_copy(c, j).wait_send()

        return 0

    lax.fori_loop(0, nz, drain, 0)


def solution(mesh):
    n_pairs, ns = mesh.shape["pairs"], mesh.shape["sect"]
    nx = x_size(n_pairs)
    nz = n_pairs // nx

    def local(wavefunction, left_normal, left_comp, right_comp, right_normal, pair_shift, pair_count, sector_rows):
        pair_dev, sec_dev, width, _ = left_normal.shape
        blocks, cols = right_comp.shape[1], right_comp.shape[2]
        chunk = sec_dev * width // nz
        part = chunk // nx
        dma = pltpu.SemaphoreType.DMA
        smem = pl.BlockSpec(memory_space=pltpu.SMEM)
        hbm = pl.BlockSpec(memory_space=pl.ANY)
        return pl.pallas_call(
            functools.partial(kernel, nz, nx, ns),
            out_shape=jax.ShapeDtypeStruct((part, blocks * cols), BF16),
            in_specs=[smem] * 3 + [hbm] * 5,
            out_specs=pl.BlockSpec(memory_space=pltpu.VMEM),
            scratch_shapes=[
                pltpu.VMEM((sec_dev + 1, width, blocks * cols), BF16),
                pltpu.VMEM((2, pair_dev, sec_dev, width, width), BF16),
                pltpu.VMEM((2, pair_dev, blocks, cols, cols), BF16),
                pltpu.VMEM((blocks, 2, pair_dev, chunk, cols), BF16),
                pltpu.VMEM((chunk, cols), F32),
                pltpu.VMEM((nz, blocks, part, cols), F32),
                pltpu.VMEM((nz, nx - 1, blocks, part, cols), BF16),
                pltpu.VMEM((nz, nx - 1, blocks, part, cols), BF16),
                pltpu.VMEM((nz, blocks, part, cols), BF16),
                pltpu.VMEM((nz, blocks, part, cols), BF16),
                pltpu.VMEM((nz // 2, blocks, part, cols), BF16),
                dma((sec_dev + 2 * sec_dev * pair_dev + 2,)),
                dma,
                dma,
                dma((nz, nx - 1, blocks)),
                dma((nz, nx - 1, blocks)),
                dma((nz, blocks)),
                dma((nz, blocks)),
                dma((nz // 2, blocks)),
            ],
            compiler_params=pltpu.CompilerParams(
                collective_id=0, has_side_effects=True, vmem_limit_bytes=62 * 2**20
            ),
        )(pair_shift, pair_count, sector_rows, wavefunction, left_normal, left_comp, right_comp, right_normal)

    placed = (
        P("sect", None),
        P("pairs", "sect", None, None),
        P("pairs", "sect", None, None),
        P("pairs", None, None, None),
        P("pairs", None, None, None),
        P("pairs"),
        P("pairs"),
        P("sect"),
    )
    return jax.shard_map(
        local, mesh=mesh, in_specs=placed, out_specs=P(("sect", "pairs"), None), check_vma=False
    )
```

```python
import functools

import jax
import jax.numpy as jnp
from jax import lax
from jax.experimental import pallas as pl
from jax.experimental.pallas import tpu as pltpu
from jax.sharding import PartitionSpec as P

MESH = pl.DeviceIdType.MESH
F32 = jnp.float32
BF16 = jnp.bfloat16
NT = (((1,), (1,)), ((), ()))


def x_size(count):
    return 1 << ((count.bit_length() - 1) // 2)


def kernel(
    nz,
    nx,
    ns,
    shift_ref,
    count_ref,
    rows_ref,
    wave,
    left_normal,
    left_comp,
    right_comp,
    right_normal,
    out_ref,
    waves,
    lefts,
    rights,
    total,
    own,
    x_out,
    x_in,
    z_out,
    z_in,
    far_in,
    load_sem,
    halo_send,
    halo_recv,
    x_send,
    x_recv,
    z_send,
    z_recv,
    far_recv,
):
    pair_dev, sec_dev, width, _ = left_normal.shape
    blocks, cols = right_comp.shape[1], right_comp.shape[2]
    chunk = sec_dev * width // nz
    part = chunk // nx
    me = lax.axis_index("pairs")
    sect = lax.axis_index("sect")
    z = me // nx
    x = lax.rem(me, nx)
    partner = z + 1 - 2 * lax.rem(z, 2)

    late = (sect > 0) & (lax.rem(sect, 2) == 0)
    mirrored = (z >= nz // 2) & jnp.logical_not(late)

    loads = {}

    def load(name, source, target):
        copy = pltpu.make_async_copy(source, target, load_sem.at[len(loads)])
        copy.start()
        loads[name] = copy

    for s in reversed(range(sec_dev)):
        load(("wave", s), wave.at[pl.ds(s * width, width)], waves.at[s + 1])
    for i in range(sec_dev):
        s = jnp.where(mirrored, i, sec_dev - 1 - i)
        for p in range(pair_dev):
            load(("normal", i, p), left_normal.at[p, s], lefts.at[0, p, s])
            load(("comp", i, p), left_comp.at[p, s], lefts.at[1, p, s])
        if i == 0:
            load("right_comp", right_comp, rights.at[0])
            load("right_normal", right_normal, rights.at[1])

    barrier = pltpu.get_barrier_semaphore()
    for d in range(1, nx):
        pl.semaphore_signal(barrier, inc=1, device_id=(z * nx + lax.rem(x + d, nx), sect), device_id_type=MESH)
    for d in range(1, nz):
        pl.semaphore_signal(barrier, inc=1, device_id=(lax.rem(z + d, nz) * nx + x, sect), device_id_type=MESH)
    for d in (1, ns - 1):
        pl.semaphore_signal(barrier, inc=1, device_id=(me, lax.rem(sect + d, ns)), device_id_type=MESH)

    def mask(s):
        loads[("wave", s)].wait()
        step = 64

        def body(i, _):
            at = pl.ds(i * step, step)
            keep = lax.broadcasted_iota(jnp.int32, (step, blocks * cols), 0) + i * step < rows_ref[s]
            value = waves[s + 1, at, :].astype(F32)
            waves[s + 1, at, :] = jnp.where(keep, value, 0.0).astype(BF16)
            return 0

        lax.fori_loop(0, width // step, body, 0)

    mask(sec_dev - 1)
    pl.semaphore_wait(barrier, nx - 1 + nz - 1 + 2)
    halo = pltpu.make_async_remote_copy(
        src_ref=waves.at[sec_dev],
        dst_ref=waves.at[0],
        send_sem=halo_send,
        recv_sem=halo_recv,
        device_id=(me, lax.rem(sect + 1, ns)),
        device_id_type=MESH,
    )

    @pl.when(sect < ns - 1)
    def _():
        halo.start()

    @pl.when(sect == 0)
    def _():
        waves[0] = jnp.zeros((width, blocks * cols), BF16)

    for s in reversed(range(sec_dev - 1)):
        mask(s)

    per_sector = nz // sec_dev

    def sector(i):
        return jnp.where(mirrored, i, sec_dev - 1 - i)

    def chunk_of(s, q):
        mine = z - s * per_sector
        inside = (mine >= 0) & (mine < per_sector)
        skip = jnp.where(q == per_sector - 1, mine, jnp.where(q < mine, q, q + 1))
        return s * per_sector + jnp.where(inside, skip, q)

    def x_copy(c, d, j):
        return pltpu.make_async_remote_copy(
            src_ref=x_out.at[c, d - 1, j],
            dst_ref=x_in.at[c, d - 1, j],
            send_sem=x_send.at[c, d - 1, j],
            recv_sem=x_recv.at[c, d - 1, j],
            device_id=(z * nx + lax.rem(x + d, nx), sect),
            device_id_type=MESH,
        )

    def z_copy(c, j):
        return pltpu.make_async_remote_copy(
            src_ref=z_out.at[c, j],
            dst_ref=z_in.at[c, j],
            send_sem=z_send.at[c, j],
            recv_sem=z_recv.at[c, j],
            device_id=(partner * nx + x, sect),
            device_id_type=MESH,
        )

    def far_copy(c, j, slot):
        return pltpu.make_async_remote_copy(
            src_ref=z_out.at[c, j],
            dst_ref=far_in.at[slot, j],
            send_sem=z_send.at[c, j],
            recv_sem=far_recv.at[slot, j],
            device_id=(c * nx + x, sect),
            device_id_type=MESH,
        )

    def combines(c):
        above = (c // 2 > z // 2) & (lax.rem(z, 2) == 1)
        below = (c // 2 < z // 2) & (lax.rem(z, 2) == 0)
        return above | below

    def add_terms(s, j, kind):
        result = None
        for p in range(pair_dev):
            block = lax.rem(j + shift_ref[p], blocks)
            picked = waves[s + 1 - kind, :, :cols]
            for o in range(1, blocks):
                picked = jnp.where(block == o, waves[s + 1 - kind, :, o * cols : (o + 1) * cols], picked)
            value = jnp.dot(lefts[kind, p, s], picked, preferred_element_type=F32)
            value = jnp.where(p < count_ref[0], value, 0.0).astype(BF16)
            term = lax.dot_general(value, rights[kind, p, j], NT, preferred_element_type=F32)
            result = term if result is None else result + term
        total[j] = result if kind == 0 else total[j] + result

    def send_x(s, j):
        def send(q, _):
            c = chunk_of(s, q)
            start = (c - s * per_sector) * chunk
            own[c, j] = total[j, pl.ds(pl.multiple_of(start + x * part, part), part), :]
            for d in range(1, nx):
                to = lax.rem(x + d, nx)
                rows = pl.ds(pl.multiple_of(start + to * part, part), part)
                x_out[c, d - 1, j] = total[j, rows, :].astype(BF16)
                x_copy(c, d, j).start()
            return 0

        lax.fori_loop(0, per_sector, send, 0)

    def x_sum(s, j):
        def add(q, _):
            c = chunk_of(s, q)
            value = own[c, j]
            for d in range(1, nx):
                x_copy(c, d, j).wait_recv()
                value = value + x_in[c, d - 1, j].astype(F32)
            own[c, j] = value

            @pl.when((c != z) & jnp.logical_not(combines(c)))
            def _():
                z_out[c, j] = value.astype(BF16)
                z_copy(c, j).start()

            return 0

        lax.fori_loop(0, per_sector, add, 0)

    def z_sum(s, j):
        def add(q, _):
            c = chunk_of(s, q)

            @pl.when((c != z) & combines(c))
            def _():
                z_copy(c, j).wait_recv()
                z_out[c, j] = (own[c, j] + z_in[c, j].astype(F32)).astype(BF16)
                far_copy(c, j, z // 2).start()

            return 0

        lax.fori_loop(0, per_sector, add, 0)

    units = sec_dev * blocks

    def step(t, _):
        i, j = t // blocks, lax.rem(t, blocks)
        s = sector(i)
        for n in range(sec_dev):

            @pl.when(t == n * blocks)
            def _():
                for p in range(pair_dev):
                    loads[("normal", n, p)].wait()
                    loads[("comp", n, p)].wait()
                if n == 0:
                    loads["right_comp"].wait()
                    loads["right_normal"].wait()

        @pl.when(t < units)
        def _():
            begin = jnp.where(i == 0, j, jnp.where(j == 0, 0, blocks))
            end = jnp.where(i == 0, j + 1, blocks)

            def normal(b, _):
                add_terms(s, b, 0)
                return 0

            lax.fori_loop(begin, end, normal, 0)

            @pl.when((s == 0) & (j == 0) & (sect > 0))
            def _():
                halo.wait_recv()

            add_terms(s, j, 1)
            send_x(s, j)

        @pl.when((t >= 1) & (t <= units))
        def _():
            x_sum(sector((t - 1) // blocks), lax.rem(t - 1, blocks))

        @pl.when(t >= 2)
        def _():
            z_sum(sector((t - 2) // blocks), lax.rem(t - 2, blocks))

        return 0

    lax.fori_loop(0, units + 2, step, 0)

    first = me * part
    row = lax.broadcasted_iota(jnp.int32, (part, cols), 0) + lax.rem(first, width)
    kept = row < rows_ref[first // width]
    for j in range(blocks):
        value = own[z, j]
        z_copy(z, j).wait_recv()
        value = value + z_in[z, j].astype(F32)
        for d in range(1, nz // 2):
            slot = lax.rem(z // 2 + d, nz // 2)
            far_copy(z, j, slot).wait_recv()
            value = value + far_in[slot, j].astype(F32)
        out_ref[:, j * cols : (j + 1) * cols] = jnp.where(kept, value, 0.0)

    @pl.when(sect < ns - 1)
    def _():
        halo.wait_send()

    def drain(c, _):
        for j in range(blocks):
            for d in range(1, nx):
                x_copy(c, d, j).wait_send()

            @pl.when(c != z)
            def _():
                z_copy(c, j).wait_send()

        return 0

    lax.fori_loop(0, nz, drain, 0)


def solution(mesh):
    n_pairs, ns = mesh.shape["pairs"], mesh.shape["sect"]
    nx = x_size(n_pairs)
    nz = n_pairs // nx

    def local(wavefunction, left_normal, left_comp, right_comp, right_normal, pair_shift, pair_count, sector_rows):
        pair_dev, sec_dev, width, _ = left_normal.shape
        blocks, cols = right_comp.shape[1], right_comp.shape[2]
        chunk = sec_dev * width // nz
        part = chunk // nx
        dma = pltpu.SemaphoreType.DMA
        smem = pl.BlockSpec(memory_space=pltpu.SMEM)
        hbm = pl.BlockSpec(memory_space=pl.ANY)
        return pl.pallas_call(
            functools.partial(kernel, nz, nx, ns),
            out_shape=jax.ShapeDtypeStruct((part, blocks * cols), F32),
            in_specs=[smem] * 3 + [hbm] * 5,
            out_specs=pl.BlockSpec(memory_space=pltpu.VMEM),
            scratch_shapes=[
                pltpu.VMEM((sec_dev + 1, width, blocks * cols), BF16),
                pltpu.VMEM((2, pair_dev, sec_dev, width, width), BF16),
                pltpu.VMEM((2, pair_dev, blocks, cols, cols), BF16),
                pltpu.VMEM((blocks, width, cols), F32),
                pltpu.VMEM((nz, blocks, part, cols), F32),
                pltpu.VMEM((nz, nx - 1, blocks, part, cols), BF16),
                pltpu.VMEM((nz, nx - 1, blocks, part, cols), BF16),
                pltpu.VMEM((nz, blocks, part, cols), BF16),
                pltpu.VMEM((nz, blocks, part, cols), BF16),
                pltpu.VMEM((nz // 2, blocks, part, cols), BF16),
                dma((sec_dev + 2 * sec_dev * pair_dev + 2,)),
                dma,
                dma,
                dma((nz, nx - 1, blocks)),
                dma((nz, nx - 1, blocks)),
                dma((nz, blocks)),
                dma((nz, blocks)),
                dma((nz // 2, blocks)),
            ],
            compiler_params=pltpu.CompilerParams(
                collective_id=0, has_side_effects=True, vmem_limit_bytes=62 * 2**20
            ),
        )(pair_shift, pair_count, sector_rows, wavefunction, left_normal, left_comp, right_comp, right_normal).astype(BF16)

    placed = (
        P("sect", None),
        P("pairs", "sect", None, None),
        P("pairs", "sect", None, None),
        P("pairs", None, None, None),
        P("pairs", None, None, None),
        P("pairs"),
        P("pairs"),
        P("sect"),
    )
    return jax.shard_map(
        local, mesh=mesh, in_specs=placed, out_specs=P(("sect", "pairs"), None), check_vma=False
    )
```

```python
import functools

import jax
import jax.numpy as jnp
from jax import lax
from jax.experimental import pallas as pl
from jax.experimental.pallas import tpu as pltpu
from jax.sharding import PartitionSpec as P

MESH = pl.DeviceIdType.MESH
F32 = jnp.float32
BF16 = jnp.bfloat16
NT = (((1,), (1,)), ((), ()))
RELAYED = 4


def x_size(count):
    return 1 << ((count.bit_length() - 1) // 2)


def kernel(
    nz,
    nx,
    ns,
    shift_ref,
    count_ref,
    rows_ref,
    wave,
    left_normal,
    left_comp,
    right_comp,
    right_normal,
    out_ref,
    waves,
    lefts,
    rights,
    total,
    own,
    x_out,
    x_in,
    z_out,
    z_in,
    far_in,
    load_sem,
    halo_send,
    halo_recv,
    x_send,
    x_recv,
    z_send,
    z_recv,
    far_recv,
):
    pair_dev, sec_dev, width, _ = left_normal.shape
    blocks, cols = right_comp.shape[1], right_comp.shape[2]
    chunk = sec_dev * width // nz
    part = chunk // nx
    me = lax.axis_index("pairs")
    sect = lax.axis_index("sect")
    z = me // nx
    x = lax.rem(me, nx)
    partner = z + 1 - 2 * lax.rem(z, 2)

    late = (sect > 0) & (lax.rem(sect, 2) == 0)
    mirrored = z >= nz // 2
    half = lax.rem(z, 2) * RELAYED

    loads = {}

    def load(name, source, target):
        copy = pltpu.make_async_copy(source, target, load_sem.at[len(loads)])
        copy.start()
        loads[name] = copy

    for s in reversed(range(sec_dev)):
        load(("wave", s), wave.at[pl.ds(s * width, width)], waves.at[s + 1])
    for i in range(sec_dev):
        s = jnp.where(mirrored, i, sec_dev - 1 - i)
        for p in range(pair_dev):
            load(("normal", i, p), left_normal.at[p, s], lefts.at[0, p, s])
            load(("comp", i, p), left_comp.at[p, s], lefts.at[1, p, s])
        if i == 0:
            load("right_comp", right_comp, rights.at[0])
            load("right_normal", right_normal, rights.at[1])

    barrier = pltpu.get_barrier_semaphore()
    for d in range(1, nx):
        pl.semaphore_signal(barrier, inc=1, device_id=(z * nx + lax.rem(x + d, nx), sect), device_id_type=MESH)
    for d in range(1, nz):
        pl.semaphore_signal(barrier, inc=1, device_id=(lax.rem(z + d, nz) * nx + x, sect), device_id_type=MESH)
    for d in (1, ns - 1):
        pl.semaphore_signal(barrier, inc=1, device_id=(me, lax.rem(sect + d, ns)), device_id_type=MESH)

    def mask(s):
        loads[("wave", s)].wait()
        step = 64

        def body(i, _):
            at = pl.ds(i * step, step)
            keep = lax.broadcasted_iota(jnp.int32, (step, blocks * cols), 0) + i * step < rows_ref[s]
            value = waves[s + 1, at, :].astype(F32)
            waves[s + 1, at, :] = jnp.where(keep, value, 0.0).astype(BF16)
            return 0

        lax.fori_loop(0, width // step, body, 0)

    mask(sec_dev - 1)
    pl.semaphore_wait(barrier, nx - 1 + nz - 1 + 2)
    piece = width // (2 * RELAYED)

    def halo_copy(r, relay):
        rows = pl.ds(pl.multiple_of(r * piece, piece), piece)
        return pltpu.make_async_remote_copy(
            src_ref=waves.at[0 if relay else sec_dev, rows],
            dst_ref=waves.at[0, rows],
            send_sem=halo_send.at[r + 2 * RELAYED if relay else r],
            recv_sem=halo_recv.at[r],
            device_id=(partner * nx + x, sect) if relay else (me, lax.rem(sect + 1, ns)),
            device_id_type=MESH,
        )

    crosses = lax.rem(sect, 2) == 1

    @pl.when(sect < ns - 1)
    def _():
        def send(r, _):
            halo_copy(r, False).start()
            return 0

        lax.fori_loop(jnp.where(crosses, half, 0), jnp.where(crosses, half + RELAYED, 2 * RELAYED), send, 0)

    @pl.when(sect == 0)
    def _():
        waves[0] = jnp.zeros((width, blocks * cols), BF16)

    for s in reversed(range(sec_dev - 1)):
        mask(s)

    per_sector = nz // sec_dev

    def sector(i):
        return jnp.where(mirrored, i, sec_dev - 1 - i)

    def chunk_of(s, q):
        mine = z - s * per_sector
        inside = (mine >= 0) & (mine < per_sector)
        skip = jnp.where(q == per_sector - 1, mine, jnp.where(q < mine, q, q + 1))
        return s * per_sector + jnp.where(inside, skip, q)

    def x_copy(c, d, j):
        return pltpu.make_async_remote_copy(
            src_ref=x_out.at[c, d - 1, j],
            dst_ref=x_in.at[c, d - 1, j],
            send_sem=x_send.at[c, d - 1, j],
            recv_sem=x_recv.at[c, d - 1, j],
            device_id=(z * nx + lax.rem(x + d, nx), sect),
            device_id_type=MESH,
        )

    def z_copy(c, j):
        return pltpu.make_async_remote_copy(
            src_ref=z_out.at[c, j],
            dst_ref=z_in.at[c, j],
            send_sem=z_send.at[c, j],
            recv_sem=z_recv.at[c, j],
            device_id=(partner * nx + x, sect),
            device_id_type=MESH,
        )

    def far_copy(c, j, slot):
        return pltpu.make_async_remote_copy(
            src_ref=z_out.at[c, j],
            dst_ref=far_in.at[slot, j],
            send_sem=z_send.at[c, j],
            recv_sem=far_recv.at[slot, j],
            device_id=(c * nx + x, sect),
            device_id_type=MESH,
        )

    def combines(c):
        above = (c // 2 > z // 2) & (lax.rem(z, 2) == 1)
        below = (c // 2 < z // 2) & (lax.rem(z, 2) == 0)
        return above | below

    def add_terms(s, j, kind):
        result = None
        for p in range(pair_dev):
            block = lax.rem(j + shift_ref[p], blocks)
            picked = waves[s + 1 - kind, :, :cols]
            for o in range(1, blocks):
                picked = jnp.where(block == o, waves[s + 1 - kind, :, o * cols : (o + 1) * cols], picked)
            value = jnp.dot(lefts[kind, p, s], picked, preferred_element_type=F32)
            value = jnp.where(p < count_ref[0], value, 0.0).astype(BF16)
            term = lax.dot_general(value, rights[kind, p, j], NT, preferred_element_type=F32)
            result = term if result is None else result + term
        total[j] = result if kind == 0 else total[j] + result

    def send_x(s, j):
        def send(q, _):
            c = chunk_of(s, q)
            start = (c - s * per_sector) * chunk
            own[c, j] = total[j, pl.ds(pl.multiple_of(start + x * part, part), part), :]
            for d in range(1, nx):
                to = lax.rem(x + d, nx)
                rows = pl.ds(pl.multiple_of(start + to * part, part), part)
                x_out[c, d - 1, j] = total[j, rows, :].astype(BF16)
                x_copy(c, d, j).start()
            return 0

        lax.fori_loop(0, per_sector, send, 0)

    def x_sum(s, j):
        def add(q, _):
            c = chunk_of(s, q)
            value = own[c, j]
            for d in range(1, nx):
                x_copy(c, d, j).wait_recv()
                value = value + x_in[c, d - 1, j].astype(F32)
            own[c, j] = value

            @pl.when((c != z) & jnp.logical_not(combines(c)))
            def _():
                z_out[c, j] = value.astype(BF16)
                z_copy(c, j).start()

            return 0

        lax.fori_loop(0, per_sector, add, 0)

    def z_sum(s, j):
        def add(q, _):
            c = chunk_of(s, q)

            @pl.when((c != z) & combines(c))
            def _():
                z_copy(c, j).wait_recv()
                z_out[c, j] = (own[c, j] + z_in[c, j].astype(F32)).astype(BF16)
                far_copy(c, j, z // 2).start()

            return 0

        lax.fori_loop(0, per_sector, add, 0)

    units = sec_dev * blocks

    def step(t, _):
        i, j = t // blocks, lax.rem(t, blocks)
        s = sector(i)
        for n in range(sec_dev):

            @pl.when(t == n * blocks)
            def _():
                for p in range(pair_dev):
                    loads[("normal", n, p)].wait()
                    loads[("comp", n, p)].wait()
                if n == 0:
                    loads["right_comp"].wait()
                    loads["right_normal"].wait()

        @pl.when(t < units)
        def _():
            single = (i == 0) & jnp.logical_not(late)
            begin = jnp.where(single, j, jnp.where(j == 0, 0, blocks))
            end = jnp.where(single, j + 1, blocks)

            def normal(b, _):
                add_terms(s, b, 0)

                @pl.when((t == 0) & late)
                def _():
                    each = RELAYED // blocks
                    for r in range(each):
                        at = half + b * each + r
                        halo_copy(at, False).wait_recv()
                        halo_copy(at, True).start()

                return 0

            lax.fori_loop(begin, end, normal, 0)

            @pl.when((s == 0) & (j == 0) & (sect > 0))
            def _():
                other = RELAYED - half

                def wait(r, _):
                    halo_copy(r, False).wait_recv()
                    return 0

                lax.fori_loop(jnp.where(late, other, 0), jnp.where(late, other + RELAYED, 2 * RELAYED), wait, 0)

            add_terms(s, j, 1)
            send_x(s, j)

        @pl.when((t >= 1) & (t <= units))
        def _():
            x_sum(sector((t - 1) // blocks), lax.rem(t - 1, blocks))

        @pl.when(t >= 2)
        def _():
            z_sum(sector((t - 2) // blocks), lax.rem(t - 2, blocks))

        return 0

    lax.fori_loop(0, units + 2, step, 0)

    first = me * part
    row = lax.broadcasted_iota(jnp.int32, (part, cols), 0) + lax.rem(first, width)
    kept = row < rows_ref[first // width]
    for j in range(blocks):
        value = own[z, j]
        z_copy(z, j).wait_recv()
        value = value + z_in[z, j].astype(F32)
        for d in range(1, nz // 2):
            slot = lax.rem(z // 2 + d, nz // 2)
            far_copy(z, j, slot).wait_recv()
            value = value + far_in[slot, j].astype(F32)
        out_ref[:, j * cols : (j + 1) * cols] = jnp.where(kept, value, 0.0)

    @pl.when(sect < ns - 1)
    def _():
        def sent(r, _):
            halo_copy(r, False).wait_send()
            return 0

        lax.fori_loop(jnp.where(crosses, half, 0), jnp.where(crosses, half + RELAYED, 2 * RELAYED), sent, 0)

    @pl.when(late)
    def _():
        def sent(r, _):
            halo_copy(r, True).wait_send()
            return 0

        lax.fori_loop(half, half + RELAYED, sent, 0)

    def drain(c, _):
        for j in range(blocks):
            for d in range(1, nx):
                x_copy(c, d, j).wait_send()

            @pl.when(c != z)
            def _():
                z_copy(c, j).wait_send()

        return 0

    lax.fori_loop(0, nz, drain, 0)


def solution(mesh):
    n_pairs, ns = mesh.shape["pairs"], mesh.shape["sect"]
    nx = x_size(n_pairs)
    nz = n_pairs // nx

    def local(wavefunction, left_normal, left_comp, right_comp, right_normal, pair_shift, pair_count, sector_rows):
        pair_dev, sec_dev, width, _ = left_normal.shape
        blocks, cols = right_comp.shape[1], right_comp.shape[2]
        chunk = sec_dev * width // nz
        part = chunk // nx
        dma = pltpu.SemaphoreType.DMA
        smem = pl.BlockSpec(memory_space=pltpu.SMEM)
        hbm = pl.BlockSpec(memory_space=pl.ANY)
        return pl.pallas_call(
            functools.partial(kernel, nz, nx, ns),
            out_shape=jax.ShapeDtypeStruct((part, blocks * cols), F32),
            in_specs=[smem] * 3 + [hbm] * 5,
            out_specs=pl.BlockSpec(memory_space=pltpu.VMEM),
            scratch_shapes=[
                pltpu.VMEM((sec_dev + 1, width, blocks * cols), BF16),
                pltpu.VMEM((2, pair_dev, sec_dev, width, width), BF16),
                pltpu.VMEM((2, pair_dev, blocks, cols, cols), BF16),
                pltpu.VMEM((blocks, width, cols), F32),
                pltpu.VMEM((nz, blocks, part, cols), F32),
                pltpu.VMEM((nz, nx - 1, blocks, part, cols), BF16),
                pltpu.VMEM((nz, nx - 1, blocks, part, cols), BF16),
                pltpu.VMEM((nz, blocks, part, cols), BF16),
                pltpu.VMEM((nz, blocks, part, cols), BF16),
                pltpu.VMEM((nz // 2, blocks, part, cols), BF16),
                dma((sec_dev + 2 * sec_dev * pair_dev + 2,)),
                dma((4 * RELAYED,)),
                dma((2 * RELAYED,)),
                dma((nz, nx - 1, blocks)),
                dma((nz, nx - 1, blocks)),
                dma((nz, blocks)),
                dma((nz, blocks)),
                dma((nz // 2, blocks)),
            ],
            compiler_params=pltpu.CompilerParams(
                collective_id=0, has_side_effects=True, vmem_limit_bytes=61 * 2**20
            ),
        )(pair_shift, pair_count, sector_rows, wavefunction, left_normal, left_comp, right_comp, right_normal).astype(BF16)

    placed = (
        P("sect", None),
        P("pairs", "sect", None, None),
        P("pairs", "sect", None, None),
        P("pairs", None, None, None),
        P("pairs", None, None, None),
        P("pairs"),
        P("pairs"),
        P("sect"),
    )
    return jax.shard_map(
        local, mesh=mesh, in_specs=placed, out_specs=P(("sect", "pairs"), None), check_vma=False
    )
```

```python
import functools

import jax
import jax.numpy as jnp
from jax import lax
from jax.experimental import pallas as pl
from jax.experimental.pallas import tpu as pltpu
from jax.sharding import PartitionSpec as P

MESH = pl.DeviceIdType.MESH
F32 = jnp.float32
BF16 = jnp.bfloat16
NT = (((1,), (1,)), ((), ()))


def x_size(count):
    return 1 << ((count.bit_length() - 1) // 2)


def kernel(
    nz,
    nx,
    ns,
    shift_ref,
    count_ref,
    rows_ref,
    wave,
    left_normal,
    left_comp,
    right_comp,
    right_normal,
    out_ref,
    waves,
    relay,
    lefts,
    rights,
    total,
    own,
    x_out,
    x_in,
    z_out,
    z_in,
    far_in,
    load_sem,
    halo_send,
    halo_recv,
    x_send,
    x_recv,
    z_send,
    z_recv,
    far_recv,
):
    pair_dev, sec_dev, width, _ = left_normal.shape
    blocks, cols = right_comp.shape[1], right_comp.shape[2]
    chunk = sec_dev * width // nz
    part = chunk // nx
    me = lax.axis_index("pairs")
    sect = lax.axis_index("sect")
    z = me // nx
    x = lax.rem(me, nx)
    partner = z + 1 - 2 * lax.rem(z, 2)

    late = (sect > 0) & (lax.rem(sect, 2) == 0)
    mirrored = (z >= nz // 2) & jnp.logical_not(late)

    loads = {}

    def load(name, source, target):
        copy = pltpu.make_async_copy(source, target, load_sem.at[len(loads)])
        copy.start()
        loads[name] = copy

    for s in reversed(range(sec_dev)):
        load(("wave", s), wave.at[pl.ds(s * width, width)], waves.at[s + 1])
    for i in range(sec_dev):
        s = jnp.where(mirrored, i, sec_dev - 1 - i)
        for p in range(pair_dev):
            load(("normal", i, p), left_normal.at[p, s], lefts.at[0, p, s])
            load(("comp", i, p), left_comp.at[p, s], lefts.at[1, p, s])
        if i == 0:
            load("right_comp", right_comp, rights.at[0])
            load("right_normal", right_normal, rights.at[1])

    barrier = pltpu.get_barrier_semaphore()
    for d in range(1, nx):
        pl.semaphore_signal(barrier, inc=1, device_id=(z * nx + lax.rem(x + d, nx), sect), device_id_type=MESH)
    for d in range(1, nz):
        pl.semaphore_signal(barrier, inc=1, device_id=(lax.rem(z + d, nz) * nx + x, sect), device_id_type=MESH)
    for d in (1, ns - 1, 2, ns - 2):
        pl.semaphore_signal(barrier, inc=1, device_id=(me, lax.rem(sect + d, ns)), device_id_type=MESH)

    def mask(s):
        loads[("wave", s)].wait()
        step = 64

        def body(i, _):
            at = pl.ds(i * step, step)
            keep = lax.broadcasted_iota(jnp.int32, (step, blocks * cols), 0) + i * step < rows_ref[s]
            value = waves[s + 1, at, :].astype(F32)
            waves[s + 1, at, :] = jnp.where(keep, value, 0.0).astype(BF16)
            return 0

        lax.fori_loop(0, width // step, body, 0)

    mask(sec_dev - 1)
    pl.semaphore_wait(barrier, nx - 1 + nz - 1 + 4)
    top, bottom = pl.ds(0, width // 2), pl.ds(width // 2, width // 2)

    def halo_copy(n, source, rows, target, to):
        return pltpu.make_async_remote_copy(
            src_ref=source.at[rows],
            dst_ref=target.at[rows],
            send_sem=halo_send.at[n],
            recv_sem=halo_recv.at[n],
            device_id=(me, lax.rem(to, ns)),
            device_id_type=MESH,
        )

    odd = lax.rem(sect, 2) == 1
    sends, crosses = sect < ns - 1, (sect < ns - 1) & odd
    relays = (sect < ns - 2) & jnp.logical_not(odd)
    held = relay.at[0]
    top_copy = halo_copy(0, waves.at[sec_dev], top, waves.at[0], sect + 1)
    bottom_copy = halo_copy(1, waves.at[sec_dev], bottom, waves.at[0], sect + 1)
    back_copy = halo_copy(2, waves.at[sec_dev], bottom, held, sect + ns - 1)
    relay_copy = halo_copy(3, held, bottom, waves.at[0], sect + 2)

    @pl.when(crosses)
    def _():
        back_copy.start()

    @pl.when(sends)
    def _():
        top_copy.start()

    @pl.when(sends & jnp.logical_not(odd))
    def _():
        bottom_copy.start()

    @pl.when(sect == 0)
    def _():
        waves[0] = jnp.zeros((width, blocks * cols), BF16)

    for s in reversed(range(sec_dev - 1)):
        mask(s)

    per_sector = nz // sec_dev

    def sector(i):
        return jnp.where(mirrored, i, sec_dev - 1 - i)

    def chunk_of(s, q):
        mine = z - s * per_sector
        inside = (mine >= 0) & (mine < per_sector)
        skip = jnp.where(q == per_sector - 1, mine, jnp.where(q < mine, q, q + 1))
        return s * per_sector + jnp.where(inside, skip, q)

    def x_copy(c, d, j):
        return pltpu.make_async_remote_copy(
            src_ref=x_out.at[c, d - 1, j],
            dst_ref=x_in.at[c, d - 1, j],
            send_sem=x_send.at[c, d - 1, j],
            recv_sem=x_recv.at[c, d - 1, j],
            device_id=(z * nx + lax.rem(x + d, nx), sect),
            device_id_type=MESH,
        )

    def z_copy(c, j):
        return pltpu.make_async_remote_copy(
            src_ref=z_out.at[c, j],
            dst_ref=z_in.at[c, j],
            send_sem=z_send.at[c, j],
            recv_sem=z_recv.at[c, j],
            device_id=(partner * nx + x, sect),
            device_id_type=MESH,
        )

    def far_copy(c, j, slot):
        return pltpu.make_async_remote_copy(
            src_ref=z_out.at[c, j],
            dst_ref=far_in.at[slot, j],
            send_sem=z_send.at[c, j],
            recv_sem=far_recv.at[slot, j],
            device_id=(c * nx + x, sect),
            device_id_type=MESH,
        )

    def combines(c):
        above = (c // 2 > z // 2) & (lax.rem(z, 2) == 1)
        below = (c // 2 < z // 2) & (lax.rem(z, 2) == 0)
        return above | below

    def add_terms(s, j, kind):
        result = None
        for p in range(pair_dev):
            block = lax.rem(j + shift_ref[p], blocks)
            picked = waves[s + 1 - kind, :, :cols]
            for o in range(1, blocks):
                picked = jnp.where(block == o, waves[s + 1 - kind, :, o * cols : (o + 1) * cols], picked)
            value = jnp.dot(lefts[kind, p, s], picked, preferred_element_type=F32)
            value = jnp.where(p < count_ref[0], value, 0.0).astype(BF16)
            term = lax.dot_general(value, rights[kind, p, j], NT, preferred_element_type=F32)
            result = term if result is None else result + term
        total[j] = result if kind == 0 else total[j] + result

    def send_x(s, j):
        def send(q, _):
            c = chunk_of(s, q)
            start = (c - s * per_sector) * chunk
            own[c, j] = total[j, pl.ds(pl.multiple_of(start + x * part, part), part), :]
            for d in range(1, nx):
                to = lax.rem(x + d, nx)
                rows = pl.ds(pl.multiple_of(start + to * part, part), part)
                x_out[c, d - 1, j] = total[j, rows, :].astype(BF16)
                x_copy(c, d, j).start()
            return 0

        lax.fori_loop(0, per_sector, send, 0)

    def x_sum(s, j):
        def add(q, _):
            c = chunk_of(s, q)
            value = own[c, j]
            for d in range(1, nx):
                x_copy(c, d, j).wait_recv()
                value = value + x_in[c, d - 1, j].astype(F32)
            own[c, j] = value

            @pl.when((c != z) & jnp.logical_not(combines(c)))
            def _():
                z_out[c, j] = value.astype(BF16)
                z_copy(c, j).start()

            return 0

        lax.fori_loop(0, per_sector, add, 0)

    def z_sum(s, j):
        def add(q, _):
            c = chunk_of(s, q)

            @pl.when((c != z) & combines(c))
            def _():
                z_copy(c, j).wait_recv()
                z_out[c, j] = (own[c, j] + z_in[c, j].astype(F32)).astype(BF16)
                far_copy(c, j, z // 2).start()

            return 0

        lax.fori_loop(0, per_sector, add, 0)

    units = sec_dev * blocks

    def step(t, _):
        i, j = t // blocks, lax.rem(t, blocks)
        s = sector(i)
        for n in range(sec_dev):

            @pl.when(t == n * blocks)
            def _():
                for p in range(pair_dev):
                    loads[("normal", n, p)].wait()
                    loads[("comp", n, p)].wait()
                if n == 0:
                    loads["right_comp"].wait()
                    loads["right_normal"].wait()

        @pl.when(t < units)
        def _():
            begin = jnp.where(i == 0, j, jnp.where(j == 0, 0, blocks))
            end = jnp.where(i == 0, j + 1, blocks)

            def normal(b, _):
                add_terms(s, b, 0)

                @pl.when((t == 0) & relays)
                def _():
                    back_copy.wait_recv()
                    relay_copy.start()

                return 0

            lax.fori_loop(begin, end, normal, 0)

            @pl.when((s == 0) & (j == 0) & (sect > 0))
            def _():
                top_copy.wait_recv()

                @pl.when(odd)
                def _():
                    bottom_copy.wait_recv()

                @pl.when(late)
                def _():
                    relay_copy.wait_recv()

            add_terms(s, j, 1)
            send_x(s, j)

        @pl.when((t >= 1) & (t <= units))
        def _():
            x_sum(sector((t - 1) // blocks), lax.rem(t - 1, blocks))

        @pl.when(t >= 2)
        def _():
            z_sum(sector((t - 2) // blocks), lax.rem(t - 2, blocks))

        return 0

    lax.fori_loop(0, units + 2, step, 0)

    first = me * part
    row = lax.broadcasted_iota(jnp.int32, (part, cols), 0) + lax.rem(first, width)
    kept = row < rows_ref[first // width]
    for j in range(blocks):
        value = own[z, j]
        z_copy(z, j).wait_recv()
        value = value + z_in[z, j].astype(F32)
        for d in range(1, nz // 2):
            slot = lax.rem(z // 2 + d, nz // 2)
            far_copy(z, j, slot).wait_recv()
            value = value + far_in[slot, j].astype(F32)
        out_ref[:, j * cols : (j + 1) * cols] = jnp.where(kept, value, 0.0)

    @pl.when(crosses)
    def _():
        back_copy.wait_send()

    @pl.when(sends)
    def _():
        top_copy.wait_send()

    @pl.when(sends & jnp.logical_not(odd))
    def _():
        bottom_copy.wait_send()

    @pl.when(relays)
    def _():
        relay_copy.wait_send()

    def drain(c, _):
        for j in range(blocks):
            for d in range(1, nx):
                x_copy(c, d, j).wait_send()

            @pl.when(c != z)
            def _():
                z_copy(c, j).wait_send()

        return 0

    lax.fori_loop(0, nz, drain, 0)


def solution(mesh):
    n_pairs, ns = mesh.shape["pairs"], mesh.shape["sect"]
    nx = x_size(n_pairs)
    nz = n_pairs // nx

    def local(wavefunction, left_normal, left_comp, right_comp, right_normal, pair_shift, pair_count, sector_rows):
        pair_dev, sec_dev, width, _ = left_normal.shape
        blocks, cols = right_comp.shape[1], right_comp.shape[2]
        chunk = sec_dev * width // nz
        part = chunk // nx
        dma = pltpu.SemaphoreType.DMA
        smem = pl.BlockSpec(memory_space=pltpu.SMEM)
        hbm = pl.BlockSpec(memory_space=pltpu.HBM)
        return pl.pallas_call(
            functools.partial(kernel, nz, nx, ns),
            out_shape=jax.ShapeDtypeStruct((part, blocks * cols), F32),
            in_specs=[smem] * 3 + [hbm] * 5,
            out_specs=pl.BlockSpec(memory_space=pltpu.VMEM),
            scratch_shapes=[
                pltpu.VMEM((sec_dev + 1, width, blocks * cols), BF16),
                pltpu.VMEM((1, width, blocks * cols), BF16),
                pltpu.VMEM((2, pair_dev, sec_dev, width, width), BF16),
                pltpu.VMEM((2, pair_dev, blocks, cols, cols), BF16),
                pltpu.VMEM((blocks, width, cols), F32),
                pltpu.VMEM((nz, blocks, part, cols), F32),
                pltpu.VMEM((nz, nx - 1, blocks, part, cols), BF16),
                pltpu.VMEM((nz, nx - 1, blocks, part, cols), BF16),
                pltpu.VMEM((nz, blocks, part, cols), BF16),
                pltpu.VMEM((nz, blocks, part, cols), BF16),
                pltpu.VMEM((nz // 2, blocks, part, cols), BF16),
                dma((sec_dev + 2 * sec_dev * pair_dev + 2,)),
                dma((4,)),
                dma((4,)),
                dma((nz, nx - 1, blocks)),
                dma((nz, nx - 1, blocks)),
                dma((nz, blocks)),
                dma((nz, blocks)),
                dma((nz // 2, blocks)),
            ],
            compiler_params=pltpu.CompilerParams(
                collective_id=0, has_side_effects=True, vmem_limit_bytes=60 * 2**20
            ),
        )(pair_shift, pair_count, sector_rows, wavefunction, left_normal, left_comp, right_comp, right_normal).astype(BF16)

    placed = (
        P("sect", None),
        P("pairs", "sect", None, None),
        P("pairs", "sect", None, None),
        P("pairs", None, None, None),
        P("pairs", None, None, None),
        P("pairs"),
        P("pairs"),
        P("sect"),
    )
    return jax.shard_map(
        local, mesh=mesh, in_specs=placed, out_specs=P(("sect", "pairs"), None), check_vma=False
    )
```

```python
import functools

import jax
import jax.numpy as jnp
from jax import lax
from jax.experimental import pallas as pl
from jax.experimental.pallas import tpu as pltpu
from jax.sharding import PartitionSpec as P

MESH = pl.DeviceIdType.MESH
F32 = jnp.float32
BF16 = jnp.bfloat16
NT = (((1,), (1,)), ((), ()))


def x_size(count):
    return 1 << ((count.bit_length() - 1) // 2)


def kernel(
    nz,
    nx,
    ns,
    shift_ref,
    count_ref,
    rows_ref,
    wave,
    left_normal,
    left_comp,
    right_comp,
    right_normal,
    out_ref,
    waves,
    lefts,
    rights,
    total,
    own,
    x_out,
    x_in,
    z_out,
    z_in,
    far_in,
    load_sem,
    halo_send,
    halo_recv,
    x_send,
    x_recv,
    z_send,
    z_recv,
    far_recv,
):
    pair_dev, sec_dev, width, _ = left_normal.shape
    blocks, cols = right_comp.shape[1], right_comp.shape[2]
    chunk = sec_dev * width // nz
    part = chunk // nx
    me = lax.axis_index("pairs")
    sect = lax.axis_index("sect")
    z = me // nx
    x = lax.rem(me, nx)
    partner = z + 1 - 2 * lax.rem(z, 2)

    late = (sect > 0) & (lax.rem(sect, 2) == 0)
    mirrored = (z >= nz // 2) & jnp.logical_not(late)

    loads = {}

    def load(name, source, target):
        copy = pltpu.make_async_copy(source, target, load_sem.at[len(loads)])
        copy.start()
        loads[name] = copy

    for s in reversed(range(sec_dev)):
        load(("wave", s), wave.at[pl.ds(s * width, width)], waves.at[s + 1])
    for i in range(sec_dev):
        s = jnp.where(mirrored, i, sec_dev - 1 - i)
        for p in range(pair_dev):
            load(("normal", i, p), left_normal.at[p, s], lefts.at[0, p, s])
        if i == 0:
            load("right_comp", right_comp, rights.at[0])
        for p in range(pair_dev):
            load(("comp", i, p), left_comp.at[p, s], lefts.at[1, p, s])
        if i == 0:
            load("right_normal", right_normal, rights.at[1])

    barrier = pltpu.get_barrier_semaphore()
    for d in range(1, nx):
        pl.semaphore_signal(barrier, inc=1, device_id=(z * nx + lax.rem(x + d, nx), sect), device_id_type=MESH)
    for d in range(1, nz):
        pl.semaphore_signal(barrier, inc=1, device_id=(lax.rem(z + d, nz) * nx + x, sect), device_id_type=MESH)
    for d in (1, ns - 1):
        pl.semaphore_signal(barrier, inc=1, device_id=(me, lax.rem(sect + d, ns)), device_id_type=MESH)

    def mask(s):
        loads[("wave", s)].wait()
        step = 64

        def body(i, _):
            at = pl.ds(i * step, step)
            row = lax.broadcasted_iota(jnp.int32, (step, 128), 0) + i * step
            keep = jnp.where(row < rows_ref[s], 1.0, 0.0).astype(BF16)
            for first in range(0, blocks * cols, 128):
                columns = slice(first, first + 128)
                waves[s + 1, at, columns] = waves[s + 1, at, columns] * keep
            return 0

        lax.fori_loop(0, width // step, body, 0)

    mask(sec_dev - 1)
    pl.semaphore_wait(barrier, nx - 1 + nz - 1 + 2)
    halo = pltpu.make_async_remote_copy(
        src_ref=waves.at[sec_dev],
        dst_ref=waves.at[0],
        send_sem=halo_send,
        recv_sem=halo_recv,
        device_id=(me, lax.rem(sect + 1, ns)),
        device_id_type=MESH,
    )

    @pl.when(sect < ns - 1)
    def _():
        halo.start()

    @pl.when(sect == 0)
    def _():
        waves[0] = jnp.zeros((width, blocks * cols), BF16)

    for s in reversed(range(sec_dev - 1)):
        mask(s)

    per_sector = nz // sec_dev

    def sector(i):
        return jnp.where(mirrored, i, sec_dev - 1 - i)

    def chunk_of(s, q):
        mine = z - s * per_sector
        inside = (mine >= 0) & (mine < per_sector)
        skip = jnp.where(q == per_sector - 1, mine, jnp.where(q < mine, q, q + 1))
        return s * per_sector + jnp.where(inside, skip, q)

    def x_copy(c, d, j):
        return pltpu.make_async_remote_copy(
            src_ref=x_out.at[c, d - 1, j],
            dst_ref=x_in.at[c, d - 1, j],
            send_sem=x_send.at[c, d - 1, j],
            recv_sem=x_recv.at[c, d - 1, j],
            device_id=(z * nx + lax.rem(x + d, nx), sect),
            device_id_type=MESH,
        )

    def z_copy(c, j):
        return pltpu.make_async_remote_copy(
            src_ref=z_out.at[c, j],
            dst_ref=z_in.at[c, j],
            send_sem=z_send.at[c, j],
            recv_sem=z_recv.at[c, j],
            device_id=(partner * nx + x, sect),
            device_id_type=MESH,
        )

    def far_copy(c, j, slot):
        return pltpu.make_async_remote_copy(
            src_ref=z_out.at[c, j],
            dst_ref=far_in.at[slot, j],
            send_sem=z_send.at[c, j],
            recv_sem=far_recv.at[slot, j],
            device_id=(c * nx + x, sect),
            device_id_type=MESH,
        )

    def combines(c):
        above = (c // 2 > z // 2) & (lax.rem(z, 2) == 1)
        below = (c // 2 < z // 2) & (lax.rem(z, 2) == 0)
        return above | below

    def add_terms(s, j, kind):
        result = None
        for p in range(pair_dev):
            block = lax.rem(j + shift_ref[p], blocks)
            picked = waves[s + 1 - kind, :, :cols]
            for o in range(1, blocks):
                picked = jnp.where(block == o, waves[s + 1 - kind, :, o * cols : (o + 1) * cols], picked)
            value = jnp.dot(lefts[kind, p, s], picked, preferred_element_type=F32)
            value = jnp.where(p < count_ref[0], value, 0.0).astype(BF16)
            term = lax.dot_general(value, rights[kind, p, j], NT, preferred_element_type=F32)
            result = term if result is None else result + term
        total[j] = result if kind == 0 else total[j] + result

    def send_x(s, j):
        def send(q, _):
            c = chunk_of(s, q)
            start = (c - s * per_sector) * chunk
            own[c, j] = total[j, pl.ds(pl.multiple_of(start + x * part, part), part), :]
            for d in range(1, nx):
                to = lax.rem(x + d, nx)
                rows = pl.ds(pl.multiple_of(start + to * part, part), part)
                x_out[c, d - 1, j] = total[j, rows, :].astype(BF16)
                x_copy(c, d, j).start()
            return 0

        lax.fori_loop(0, per_sector, send, 0)

    def x_sum(s, j):
        def add(q, _):
            c = chunk_of(s, q)
            value = own[c, j]
            for d in range(1, nx):
                x_copy(c, d, j).wait_recv()
                value = value + x_in[c, d - 1, j].astype(F32)
            own[c, j] = value

            @pl.when((c != z) & jnp.logical_not(combines(c)))
            def _():
                z_out[c, j] = value.astype(BF16)
                z_copy(c, j).start()

            return 0

        lax.fori_loop(0, per_sector, add, 0)

    def z_sum(s, j):
        def add(q, _):
            c = chunk_of(s, q)

            @pl.when((c != z) & combines(c))
            def _():
                z_copy(c, j).wait_recv()
                z_out[c, j] = (own[c, j] + z_in[c, j].astype(F32)).astype(BF16)
                far_copy(c, j, z // 2).start()

            return 0

        lax.fori_loop(0, per_sector, add, 0)

    units = sec_dev * blocks
    moved = late & (z >= nz // 2)

    def unit(t):
        there = jnp.where(t == 0, 0, jnp.where(t == units - 1, 1, t + 1))
        index = jnp.where(moved, there, t)
        return index // blocks, lax.rem(index, blocks)

    def wait_loads(i, j, name, right):
        for n in range(sec_dev):

            @pl.when((i == n) & (j == 0))
            def _():
                for p in range(pair_dev):
                    loads[(name, n, p)].wait()
                if n == 0:
                    loads[right].wait()

    def step(t, _):
        i, j = unit(t)
        s = sector(i)

        @pl.when(t < units)
        def _():
            wait_loads(i, j, "normal", "right_comp")

            begin = jnp.where(i == 0, j, jnp.where(j == 0, 0, blocks))
            end = jnp.where(i == 0, j + 1, blocks)

            def normal(b, _):
                add_terms(s, b, 0)
                return 0

            lax.fori_loop(begin, end, normal, 0)
            wait_loads(i, j, "comp", "right_normal")

            @pl.when((s == 0) & (j == 0) & (sect > 0))
            def _():
                halo.wait_recv()

            add_terms(s, j, 1)
            send_x(s, j)

        @pl.when((t >= 1) & (t <= units))
        def _():
            i, j = unit(t - 1)
            x_sum(sector(i), j)

        @pl.when(t >= 2)
        def _():
            i, j = unit(t - 2)
            z_sum(sector(i), j)

        return 0

    lax.fori_loop(0, units + 2, step, 0)

    first = me * part
    row = lax.broadcasted_iota(jnp.int32, (part, cols), 0) + lax.rem(first, width)
    kept = row < rows_ref[first // width]
    for j in range(blocks):
        value = own[z, j]
        z_copy(z, j).wait_recv()
        value = value + z_in[z, j].astype(F32)
        for d in range(1, nz // 2):
            slot = lax.rem(z // 2 + d, nz // 2)
            far_copy(z, j, slot).wait_recv()
            value = value + far_in[slot, j].astype(F32)
        out_ref[:, j * cols : (j + 1) * cols] = jnp.where(kept, value, 0.0)

    @pl.when(sect < ns - 1)
    def _():
        halo.wait_send()

    def drain(c, _):
        for j in range(blocks):
            for d in range(1, nx):
                x_copy(c, d, j).wait_send()

            @pl.when(c != z)
            def _():
                z_copy(c, j).wait_send()

        return 0

    lax.fori_loop(0, nz, drain, 0)


def solution(mesh):
    n_pairs, ns = mesh.shape["pairs"], mesh.shape["sect"]
    nx = x_size(n_pairs)
    nz = n_pairs // nx

    def local(wavefunction, left_normal, left_comp, right_comp, right_normal, pair_shift, pair_count, sector_rows):
        pair_dev, sec_dev, width, _ = left_normal.shape
        blocks, cols = right_comp.shape[1], right_comp.shape[2]
        chunk = sec_dev * width // nz
        part = chunk // nx
        dma = pltpu.SemaphoreType.DMA
        smem = pl.BlockSpec(memory_space=pltpu.SMEM)
        hbm = pl.BlockSpec(memory_space=pl.ANY)
        return pl.pallas_call(
            functools.partial(kernel, nz, nx, ns),
            out_shape=jax.ShapeDtypeStruct((part, blocks * cols), F32),
            in_specs=[smem] * 3 + [hbm] * 5,
            out_specs=pl.BlockSpec(memory_space=pltpu.VMEM),
            scratch_shapes=[
                pltpu.VMEM((sec_dev + 1, width, blocks * cols), BF16),
                pltpu.VMEM((2, pair_dev, sec_dev, width, width), BF16),
                pltpu.VMEM((2, pair_dev, blocks, cols, cols), BF16),
                pltpu.VMEM((blocks, width, cols), F32),
                pltpu.VMEM((nz, blocks, part, cols), F32),
                pltpu.VMEM((nz, nx - 1, blocks, part, cols), BF16),
                pltpu.VMEM((nz, nx - 1, blocks, part, cols), BF16),
                pltpu.VMEM((nz, blocks, part, cols), BF16),
                pltpu.VMEM((nz, blocks, part, cols), BF16),
                pltpu.VMEM((nz // 2, blocks, part, cols), BF16),
                dma((sec_dev + 2 * sec_dev * pair_dev + 2,)),
                dma,
                dma,
                dma((nz, nx - 1, blocks)),
                dma((nz, nx - 1, blocks)),
                dma((nz, blocks)),
                dma((nz, blocks)),
                dma((nz // 2, blocks)),
            ],
            compiler_params=pltpu.CompilerParams(
                collective_id=0, has_side_effects=True, vmem_limit_bytes=62 * 2**20
            ),
        )(pair_shift, pair_count, sector_rows, wavefunction, left_normal, left_comp, right_comp, right_normal).astype(BF16)

    placed = (
        P("sect", None),
        P("pairs", "sect", None, None),
        P("pairs", "sect", None, None),
        P("pairs", None, None, None),
        P("pairs", None, None, None),
        P("pairs"),
        P("pairs"),
        P("sect"),
    )
    return jax.shard_map(
        local, mesh=mesh, in_specs=placed, out_specs=P(("sect", "pairs"), None), check_vma=False
    )
```

```python
import functools

import jax
import jax.numpy as jnp
from jax import lax
from jax.experimental import pallas as pl
from jax.experimental.pallas import tpu as pltpu
from jax.sharding import PartitionSpec as P

MESH = pl.DeviceIdType.MESH
F32 = jnp.float32
BF16 = jnp.bfloat16
NT = (((1,), (1,)), ((), ()))


def x_size(count):
    return 1 << ((count.bit_length() - 1) // 2)


def kernel(
    nz,
    nx,
    ns,
    shift_ref,
    count_ref,
    rows_ref,
    wave,
    left_normal,
    left_comp,
    right_comp,
    right_normal,
    out_ref,
    waves,
    lefts,
    rights,
    total,
    own,
    x_out,
    x_in,
    z_out,
    z_in,
    far_in,
    load_sem,
    halo_send,
    halo_recv,
    x_send,
    x_recv,
    z_send,
    z_recv,
    far_recv,
):
    pair_dev, sec_dev, width, _ = left_normal.shape
    blocks, cols = right_comp.shape[1], right_comp.shape[2]
    chunk = sec_dev * width // nz
    part = chunk // nx
    me = lax.axis_index("pairs")
    sect = lax.axis_index("sect")
    z = me // nx
    x = lax.rem(me, nx)
    partner = z + 1 - 2 * lax.rem(z, 2)

    late = (sect > 0) & (lax.rem(sect, 2) == 0)
    mirrored = (z >= nz // 2) & jnp.logical_not(late)

    loads = {}

    def load(name, source, target):
        copy = pltpu.make_async_copy(source, target, load_sem.at[len(loads)])
        copy.start()
        loads[name] = copy

    for s in reversed(range(sec_dev)):
        load(("wave", s), wave.at[pl.ds(s * width, width)], waves.at[s + 1])
    for i in range(sec_dev):
        s = jnp.where(mirrored, i, sec_dev - 1 - i)
        for p in range(pair_dev):
            load(("normal", i, p), left_normal.at[p, s], lefts.at[0, p, s])
        if i == 0:
            load("right_comp", right_comp, rights.at[0])
        for p in range(pair_dev):
            load(("comp", i, p), left_comp.at[p, s], lefts.at[1, p, s])
        if i == 0:
            load("right_normal", right_normal, rights.at[1])

    barrier = pltpu.get_barrier_semaphore()
    for d in range(1, nx):
        pl.semaphore_signal(barrier, inc=1, device_id=(z * nx + lax.rem(x + d, nx), sect), device_id_type=MESH)
    for d in range(1, nz):
        pl.semaphore_signal(barrier, inc=1, device_id=(lax.rem(z + d, nz) * nx + x, sect), device_id_type=MESH)
    for d in (1, ns - 1):
        pl.semaphore_signal(barrier, inc=1, device_id=(me, lax.rem(sect + d, ns)), device_id_type=MESH)

    def mask(s):
        loads[("wave", s)].wait()
        step = 64

        def body(i, _):
            at = pl.ds(i * step, step)
            row = lax.broadcasted_iota(jnp.int32, (step, 128), 0) + i * step
            keep = jnp.where(row < rows_ref[s], 1.0, 0.0).astype(BF16)
            for first in range(0, blocks * cols, 128):
                columns = slice(first, first + 128)
                waves[s + 1, at, columns] = waves[s + 1, at, columns] * keep
            return 0

        lax.fori_loop(0, width // step, body, 0)

    mask(sec_dev - 1)
    pl.semaphore_wait(barrier, nx - 1 + nz - 1 + 2)
    halo = pltpu.make_async_remote_copy(
        src_ref=waves.at[sec_dev],
        dst_ref=waves.at[0],
        send_sem=halo_send,
        recv_sem=halo_recv,
        device_id=(me, lax.rem(sect + 1, ns)),
        device_id_type=MESH,
    )

    @pl.when(sect < ns - 1)
    def _():
        halo.start()

    @pl.when(sect == 0)
    def _():
        waves[0] = jnp.zeros((width, blocks * cols), BF16)

    for s in reversed(range(sec_dev - 1)):
        mask(s)

    per_sector = nz // sec_dev

    def sector(i):
        return jnp.where(mirrored, i, sec_dev - 1 - i)

    def chunk_of(s, q):
        mine = z - s * per_sector
        inside = (mine >= 0) & (mine < per_sector)
        skip = jnp.where(q == per_sector - 1, mine, jnp.where(q < mine, q, q + 1))
        return s * per_sector + jnp.where(inside, skip, q)

    def x_copy(c, d, j):
        return pltpu.make_async_remote_copy(
            src_ref=x_out.at[c, d - 1, j],
            dst_ref=x_in.at[c, d - 1, j],
            send_sem=x_send.at[c, d - 1, j],
            recv_sem=x_recv.at[c, d - 1, j],
            device_id=(z * nx + lax.rem(x + d, nx), sect),
            device_id_type=MESH,
        )

    def z_copy(c, j):
        return pltpu.make_async_remote_copy(
            src_ref=z_out.at[c, j],
            dst_ref=z_in.at[c, j],
            send_sem=z_send.at[c, j],
            recv_sem=z_recv.at[c, j],
            device_id=(partner * nx + x, sect),
            device_id_type=MESH,
        )

    def far_copy(c, j, slot):
        return pltpu.make_async_remote_copy(
            src_ref=z_out.at[c, j],
            dst_ref=far_in.at[slot, j],
            send_sem=z_send.at[c, j],
            recv_sem=far_recv.at[slot, j],
            device_id=(c * nx + x, sect),
            device_id_type=MESH,
        )

    def combines(c):
        above = (c // 2 > z // 2) & (lax.rem(z, 2) == 1)
        below = (c // 2 < z // 2) & (lax.rem(z, 2) == 0)
        return above | below

    def add_terms(s, j, kind, rows=slice(None)):
        result = None
        for p in range(pair_dev):
            block = lax.rem(j + shift_ref[p], blocks)
            picked = waves[s + 1 - kind, :, :cols]
            for o in range(1, blocks):
                picked = jnp.where(block == o, waves[s + 1 - kind, :, o * cols : (o + 1) * cols], picked)
            value = jnp.dot(lefts[kind, p, s, rows], picked, preferred_element_type=F32)
            value = jnp.where(p < count_ref[0], value, 0.0).astype(BF16)
            term = lax.dot_general(value, rights[kind, p, j], NT, preferred_element_type=F32)
            result = term if result is None else result + term
        total[j, rows] = result if kind == 0 else total[j, rows] + result

    def send_x(s, j, q):
        c = chunk_of(s, q)
        start = (c - s * per_sector) * chunk
        own[c, j] = total[j, pl.ds(pl.multiple_of(start + x * part, part), part), :]
        for d in range(1, nx):
            to = lax.rem(x + d, nx)
            rows = pl.ds(pl.multiple_of(start + to * part, part), part)
            x_out[c, d - 1, j] = total[j, rows, :].astype(BF16)
            x_copy(c, d, j).start()

    def x_sum(s, j):
        def add(q, _):
            c = chunk_of(s, q)
            value = own[c, j]
            for d in range(1, nx):
                x_copy(c, d, j).wait_recv()
                value = value + x_in[c, d - 1, j].astype(F32)
            own[c, j] = value

            @pl.when((c != z) & jnp.logical_not(combines(c)))
            def _():
                z_out[c, j] = value.astype(BF16)
                z_copy(c, j).start()

            return 0

        lax.fori_loop(0, per_sector, add, 0)

    def z_sum(s, j):
        def add(q, _):
            c = chunk_of(s, q)

            @pl.when((c != z) & combines(c))
            def _():
                z_copy(c, j).wait_recv()
                z_out[c, j] = (own[c, j] + z_in[c, j].astype(F32)).astype(BF16)
                far_copy(c, j, z // 2).start()

            return 0

        lax.fori_loop(0, per_sector, add, 0)

    units = sec_dev * blocks
    moved = late & (z >= nz // 2)

    def unit(t):
        there = jnp.where(t == 0, 0, jnp.where(t == units - 1, 1, t + 1))
        index = jnp.where(moved, there, t)
        return index // blocks, lax.rem(index, blocks)

    def wait_loads(i, j, name, right):
        for n in range(sec_dev):

            @pl.when((i == n) & (j == 0))
            def _():
                for p in range(pair_dev):
                    loads[(name, n, p)].wait()
                if n == 0:
                    loads[right].wait()

    def step(t, _):
        i, j = unit(t)
        s = sector(i)

        def wait_halo():
            @pl.when((s == 0) & (j == 0) & (sect > 0))
            def _():
                halo.wait_recv()

        @pl.when(t == 0)
        def _():
            wait_loads(i, j, "normal", "right_comp")
            for q in range(per_sector):
                start = (chunk_of(s, q) - s * per_sector) * chunk
                rows = pl.ds(pl.multiple_of(start, chunk), chunk)
                add_terms(s, j, 0, rows)
                if q == 0:
                    wait_loads(i, j, "comp", "right_normal")
                    wait_halo()
                add_terms(s, j, 1, rows)
                send_x(s, j, q)

        @pl.when((t > 0) & (t < units))
        def _():
            wait_loads(i, j, "normal", "right_comp")

            begin = jnp.where(i == 0, j, jnp.where(j == 0, 0, blocks))
            end = jnp.where(i == 0, j + 1, blocks)

            def normal(b, _):
                add_terms(s, b, 0)
                return 0

            lax.fori_loop(begin, end, normal, 0)
            wait_loads(i, j, "comp", "right_normal")
            wait_halo()
            add_terms(s, j, 1)

            def send(q, _):
                send_x(s, j, q)
                return 0

            lax.fori_loop(0, per_sector, send, 0)

        @pl.when(t >= 2)
        def _():
            i, j = unit(t - 2)
            z_sum(sector(i), j)

        @pl.when((t >= 1) & (t <= units))
        def _():
            i, j = unit(t - 1)
            x_sum(sector(i), j)

        return 0

    lax.fori_loop(0, units + 2, step, 0)

    first = me * part
    row = lax.broadcasted_iota(jnp.int32, (part, cols), 0) + lax.rem(first, width)
    kept = row < rows_ref[first // width]
    for j in range(blocks):
        value = own[z, j]
        z_copy(z, j).wait_recv()
        value = value + z_in[z, j].astype(F32)
        for d in range(1, nz // 2):
            slot = lax.rem(z // 2 + d, nz // 2)
            far_copy(z, j, slot).wait_recv()
            value = value + far_in[slot, j].astype(F32)
        out_ref[:, j * cols : (j + 1) * cols] = jnp.where(kept, value, 0.0)

    @pl.when(sect < ns - 1)
    def _():
        halo.wait_send()

    def drain(c, _):
        for j in range(blocks):
            for d in range(1, nx):
                x_copy(c, d, j).wait_send()

            @pl.when(c != z)
            def _():
                z_copy(c, j).wait_send()

        return 0

    lax.fori_loop(0, nz, drain, 0)


def solution(mesh):
    n_pairs, ns = mesh.shape["pairs"], mesh.shape["sect"]
    nx = x_size(n_pairs)
    nz = n_pairs // nx

    def local(wavefunction, left_normal, left_comp, right_comp, right_normal, pair_shift, pair_count, sector_rows):
        pair_dev, sec_dev, width, _ = left_normal.shape
        blocks, cols = right_comp.shape[1], right_comp.shape[2]
        chunk = sec_dev * width // nz
        part = chunk // nx
        dma = pltpu.SemaphoreType.DMA
        smem = pl.BlockSpec(memory_space=pltpu.SMEM)
        hbm = pl.BlockSpec(memory_space=pl.ANY)
        return pl.pallas_call(
            functools.partial(kernel, nz, nx, ns),
            out_shape=jax.ShapeDtypeStruct((part, blocks * cols), F32),
            in_specs=[smem] * 3 + [hbm] * 5,
            out_specs=pl.BlockSpec(memory_space=pltpu.VMEM),
            scratch_shapes=[
                pltpu.VMEM((sec_dev + 1, width, blocks * cols), BF16),
                pltpu.VMEM((2, pair_dev, sec_dev, width, width), BF16),
                pltpu.VMEM((2, pair_dev, blocks, cols, cols), BF16),
                pltpu.VMEM((blocks, width, cols), F32),
                pltpu.VMEM((nz, blocks, part, cols), F32),
                pltpu.VMEM((nz, nx - 1, blocks, part, cols), BF16),
                pltpu.VMEM((nz, nx - 1, blocks, part, cols), BF16),
                pltpu.VMEM((nz, blocks, part, cols), BF16),
                pltpu.VMEM((nz, blocks, part, cols), BF16),
                pltpu.VMEM((nz // 2, blocks, part, cols), BF16),
                dma((sec_dev + 2 * sec_dev * pair_dev + 2,)),
                dma,
                dma,
                dma((nz, nx - 1, blocks)),
                dma((nz, nx - 1, blocks)),
                dma((nz, blocks)),
                dma((nz, blocks)),
                dma((nz // 2, blocks)),
            ],
            compiler_params=pltpu.CompilerParams(
                collective_id=0, has_side_effects=True, vmem_limit_bytes=62 * 2**20
            ),
        )(pair_shift, pair_count, sector_rows, wavefunction, left_normal, left_comp, right_comp, right_normal).astype(BF16)

    placed = (
        P("sect", None),
        P("pairs", "sect", None, None),
        P("pairs", "sect", None, None),
        P("pairs", None, None, None),
        P("pairs", None, None, None),
        P("pairs"),
        P("pairs"),
        P("sect"),
    )
    return jax.shard_map(
        local, mesh=mesh, in_specs=placed, out_specs=P(("sect", "pairs"), None), check_vma=False
    )
```

```python
import functools

import jax
import jax.numpy as jnp
from jax import lax
from jax.experimental import pallas as pl
from jax.experimental.pallas import tpu as pltpu
from jax.sharding import PartitionSpec as P

MESH = pl.DeviceIdType.MESH
F32 = jnp.float32
BF16 = jnp.bfloat16
NT = (((1,), (1,)), ((), ()))


def x_size(count):
    return 1 << ((count.bit_length() - 1) // 2)


def kernel(
    nz,
    nx,
    ns,
    shift_ref,
    count_ref,
    rows_ref,
    wave,
    left_normal,
    left_comp,
    right_comp,
    right_normal,
    out_ref,
    waves,
    lefts,
    rights,
    applied,
    total,
    own,
    x_out,
    x_in,
    z_out,
    z_in,
    far_in,
    load_sem,
    halo_send,
    halo_recv,
    x_send,
    x_recv,
    z_send,
    z_recv,
    far_recv,
):
    pair_dev, sec_dev, width, _ = left_normal.shape
    blocks, cols = right_comp.shape[1], right_comp.shape[2]
    chunk = sec_dev * width // nz
    part = chunk // nx
    me = lax.axis_index("pairs")
    sect = lax.axis_index("sect")
    z = me // nx
    x = lax.rem(me, nx)
    partner = z + 1 - 2 * lax.rem(z, 2)

    late = (sect > 0) & (lax.rem(sect, 2) == 0)
    mirrored = (z >= nz // 2) & jnp.logical_not(late)

    loads = {}

    def load(name, source, target):
        copy = pltpu.make_async_copy(source, target, load_sem.at[len(loads)])
        copy.start()
        loads[name] = copy

    for s in reversed(range(sec_dev)):
        load(("wave", s), wave.at[pl.ds(s * width, width)], waves.at[s + 1])
    for i in range(sec_dev):
        s = jnp.where(mirrored, i, sec_dev - 1 - i)
        for p in range(pair_dev):
            load(("normal", i, p), left_normal.at[p, s], lefts.at[0, p, s])
        for p in range(pair_dev):
            load(("comp", i, p), left_comp.at[p, s], lefts.at[1, p, s])
        if i == 0:
            load("right_comp", right_comp, rights.at[0])
            load("right_normal", right_normal, rights.at[1])

    barrier = pltpu.get_barrier_semaphore()
    for d in range(1, nx):
        pl.semaphore_signal(barrier, inc=1, device_id=(z * nx + lax.rem(x + d, nx), sect), device_id_type=MESH)
    for d in range(1, nz):
        pl.semaphore_signal(barrier, inc=1, device_id=(lax.rem(z + d, nz) * nx + x, sect), device_id_type=MESH)
    for d in (1, ns - 1):
        pl.semaphore_signal(barrier, inc=1, device_id=(me, lax.rem(sect + d, ns)), device_id_type=MESH)

    def mask(s):
        loads[("wave", s)].wait()
        step = 64

        def body(i, _):
            at = pl.ds(i * step, step)
            row = lax.broadcasted_iota(jnp.int32, (step, 128), 0) + i * step
            keep = jnp.where(row < rows_ref[s], 1.0, 0.0).astype(BF16)
            for first in range(0, blocks * cols, 128):
                columns = slice(first, first + 128)
                waves[s + 1, at, columns] = waves[s + 1, at, columns] * keep
            return 0

        lax.fori_loop(0, width // step, body, 0)

    mask(sec_dev - 1)
    pl.semaphore_wait(barrier, nx - 1 + nz - 1 + 2)
    halo = pltpu.make_async_remote_copy(
        src_ref=waves.at[sec_dev],
        dst_ref=waves.at[0],
        send_sem=halo_send,
        recv_sem=halo_recv,
        device_id=(me, lax.rem(sect + 1, ns)),
        device_id_type=MESH,
    )

    @pl.when(sect < ns - 1)
    def _():
        halo.start()

    @pl.when(sect == 0)
    def _():
        waves[0] = jnp.zeros((width, blocks * cols), BF16)

    for s in reversed(range(sec_dev - 1)):
        mask(s)

    def order(k):
        down = nz - 1 - k
        at = jnp.where(mirrored, nz - 1 - z, z)
        c = jnp.where(k == nz - 1, at, jnp.where(down > at, down, down - 1))
        return jnp.where(mirrored, nz - 1 - c, c)

    def x_copy(c, d, j):
        return pltpu.make_async_remote_copy(
            src_ref=x_out.at[c, d - 1, j],
            dst_ref=x_in.at[c, d - 1, j],
            send_sem=x_send.at[c, d - 1, j],
            recv_sem=x_recv.at[c, d - 1, j],
            device_id=(z * nx + lax.rem(x + d, nx), sect),
            device_id_type=MESH,
        )

    def z_copy(c, j):
        return pltpu.make_async_remote_copy(
            src_ref=z_out.at[c, j],
            dst_ref=z_in.at[c, j],
            send_sem=z_send.at[c, j],
            recv_sem=z_recv.at[c, j],
            device_id=(partner * nx + x, sect),
            device_id_type=MESH,
        )

    def far_copy(c, j, slot):
        return pltpu.make_async_remote_copy(
            src_ref=z_out.at[c, j],
            dst_ref=far_in.at[slot, j],
            send_sem=z_send.at[c, j],
            recv_sem=far_recv.at[slot, j],
            device_id=(c * nx + x, sect),
            device_id_type=MESH,
        )

    def combines(c):
        above = (c // 2 > z // 2) & (lax.rem(z, 2) == 1)
        below = (c // 2 < z // 2) & (lax.rem(z, 2) == 0)
        return above | below

    def wait_left(i, kind):
        for p in range(pair_dev):
            loads[(("normal", "comp")[kind], i, p)].wait()

    own_late = jnp.where(z >= nz // sec_dev, 1, 0)
    halo_step = jnp.where(mirrored, 0, nz - nz // sec_dev - own_late)

    def compute(k):
        c = order(k)
        s = c * chunk // width
        at = pl.ds(pl.multiple_of(c * chunk - s * width, chunk), chunk)
        for kind in range(2):

            @pl.when(k == 0)
            def _():
                wait_left(0, kind)

            @pl.when(k == nz // sec_dev - 1)
            def _():
                for i in range(1, sec_dev):
                    wait_left(i, kind)

            if kind == 1:

                @pl.when((k == halo_step) & (sect > 0))
                def _():
                    halo.wait_recv()

            for p in range(pair_dev):
                live = p < count_ref[0]
                offset = shift_ref[p]
                ops = lefts[kind, p, s, at, :]
                value = jnp.dot(ops, waves[s + 1 - kind], preferred_element_type=F32)
                value = jnp.where(live, value, 0.0).astype(BF16)
                pieces = [value[:, j * cols : (j + 1) * cols] for j in range(blocks)]
                for j in range(blocks):
                    piece = pieces[j]
                    for o in range(1, blocks):
                        piece = jnp.where(offset == o, pieces[(j + o) % blocks], piece)
                    applied[j, kind, p] = piece

        @pl.when(k == 0)
        def _():
            loads["right_comp"].wait()
            loads["right_normal"].wait()

        for j in range(blocks):
            result = None
            for kind in range(2):
                for p in range(pair_dev):
                    term = lax.dot_general(applied[j, kind, p], rights[kind, p, j], NT, preferred_element_type=F32)
                    result = term if result is None else result + term
            total[...] = result
            own[c, j] = total[pl.ds(pl.multiple_of(x * part, part), part), :]
            for d in range(1, nx):
                to = lax.rem(x + d, nx)
                x_out[c, d - 1, j] = total[pl.ds(pl.multiple_of(to * part, part), part), :].astype(BF16)
                x_copy(c, d, j).start()

    def x_sum(k):
        c = order(k)
        for j in range(blocks):
            value = own[c, j]
            for d in range(1, nx):
                x_copy(c, d, j).wait_recv()
                value = value + x_in[c, d - 1, j].astype(F32)
            own[c, j] = value

            @pl.when((c != z) & jnp.logical_not(combines(c)))
            def _():
                z_out[c, j] = value.astype(BF16)
                z_copy(c, j).start()

    def z_sum(k):
        c = order(k)

        @pl.when((c != z) & combines(c))
        def _():
            for j in range(blocks):
                z_copy(c, j).wait_recv()
                z_out[c, j] = (own[c, j] + z_in[c, j].astype(F32)).astype(BF16)
                far_copy(c, j, z // 2).start()

    def step(k, _):
        @pl.when(k < nz)
        def _():
            compute(k)

        @pl.when(k >= 2)
        def _():
            z_sum(k - 2)

        @pl.when((k >= 1) & (k <= nz))
        def _():
            x_sum(k - 1)

        return 0

    lax.fori_loop(0, nz + 1, step, 0)

    first = me * part
    row = lax.broadcasted_iota(jnp.int32, (part, cols), 0) + lax.rem(first, width)
    kept = row < rows_ref[first // width]
    for j in range(blocks):
        value = own[z, j]
        z_copy(z, j).wait_recv()
        value = value + z_in[z, j].astype(F32)
        for d in range(1, nz // 2):
            slot = lax.rem(z // 2 + d, nz // 2)
            far_copy(z, j, slot).wait_recv()
            value = value + far_in[slot, j].astype(F32)
        out_ref[:, j * cols : (j + 1) * cols] = jnp.where(kept, value, 0.0).astype(BF16)

    @pl.when(sect < ns - 1)
    def _():
        halo.wait_send()

    def drain(k, _):
        c = order(k)
        for j in range(blocks):
            for d in range(1, nx):
                x_copy(c, d, j).wait_send()

            @pl.when(c != z)
            def _():
                z_copy(c, j).wait_send()

        return 0

    lax.fori_loop(0, nz, drain, 0)


def solution(mesh):
    n_pairs, ns = mesh.shape["pairs"], mesh.shape["sect"]
    nx = x_size(n_pairs)
    nz = n_pairs // nx

    def local(wavefunction, left_normal, left_comp, right_comp, right_normal, pair_shift, pair_count, sector_rows):
        pair_dev, sec_dev, width, _ = left_normal.shape
        blocks, cols = right_comp.shape[1], right_comp.shape[2]
        chunk = sec_dev * width // nz
        part = chunk // nx
        dma = pltpu.SemaphoreType.DMA
        smem = pl.BlockSpec(memory_space=pltpu.SMEM)
        hbm = pl.BlockSpec(memory_space=pl.ANY)
        return pl.pallas_call(
            functools.partial(kernel, nz, nx, ns),
            out_shape=jax.ShapeDtypeStruct((part, blocks * cols), BF16),
            in_specs=[smem] * 3 + [hbm] * 5,
            out_specs=pl.BlockSpec(memory_space=pltpu.VMEM),
            scratch_shapes=[
                pltpu.VMEM((sec_dev + 1, width, blocks * cols), BF16),
                pltpu.VMEM((2, pair_dev, sec_dev, width, width), BF16),
                pltpu.VMEM((2, pair_dev, blocks, cols, cols), BF16),
                pltpu.VMEM((blocks, 2, pair_dev, chunk, cols), BF16),
                pltpu.VMEM((chunk, cols), F32),
                pltpu.VMEM((nz, blocks, part, cols), F32),
                pltpu.VMEM((nz, nx - 1, blocks, part, cols), BF16),
                pltpu.VMEM((nz, nx - 1, blocks, part, cols), BF16),
                pltpu.VMEM((nz, blocks, part, cols), BF16),
                pltpu.VMEM((nz, blocks, part, cols), BF16),
                pltpu.VMEM((nz // 2, blocks, part, cols), BF16),
                dma((sec_dev + 2 * sec_dev * pair_dev + 2,)),
                dma,
                dma,
                dma((nz, nx - 1, blocks)),
                dma((nz, nx - 1, blocks)),
                dma((nz, blocks)),
                dma((nz, blocks)),
                dma((nz // 2, blocks)),
            ],
            compiler_params=pltpu.CompilerParams(
                collective_id=0, has_side_effects=True, vmem_limit_bytes=62 * 2**20
            ),
        )(pair_shift, pair_count, sector_rows, wavefunction, left_normal, left_comp, right_comp, right_normal)

    placed = (
        P("sect", None),
        P("pairs", "sect", None, None),
        P("pairs", "sect", None, None),
        P("pairs", None, None, None),
        P("pairs", None, None, None),
        P("pairs"),
        P("pairs"),
        P("sect"),
    )
    return jax.shard_map(
        local, mesh=mesh, in_specs=placed, out_specs=P(("sect", "pairs"), None), check_vma=False
    )
```

```python
import functools

import jax
import jax.numpy as jnp
from jax import lax
from jax.experimental import pallas as pl
from jax.experimental.pallas import tpu as pltpu
from jax.sharding import PartitionSpec as P

MESH = pl.DeviceIdType.MESH
F32 = jnp.float32
BF16 = jnp.bfloat16
NT = (((1,), (1,)), ((), ()))


def x_size(count):
    return 1 << ((count.bit_length() - 1) // 2)


def kernel(
    nz,
    nx,
    ns,
    shift_ref,
    count_ref,
    rows_ref,
    wave,
    left_normal,
    left_comp,
    right_comp,
    right_normal,
    out_ref,
    waves,
    lefts,
    rights,
    applied,
    total,
    own,
    x_out,
    x_in,
    z_out,
    z_in,
    far_in,
    load_sem,
    halo_send,
    halo_recv,
    x_send,
    x_recv,
    z_send,
    z_recv,
    far_recv,
):
    pair_dev, sec_dev, width, _ = left_normal.shape
    blocks, cols = right_comp.shape[1], right_comp.shape[2]
    chunk = sec_dev * width // nz
    part = chunk // nx
    me = lax.axis_index("pairs")
    sect = lax.axis_index("sect")
    z = me // nx
    x = lax.rem(me, nx)
    partner = z + 1 - 2 * lax.rem(z, 2)

    late = (sect > 0) & (lax.rem(sect, 2) == 0)
    mirrored = (z >= nz // 2) & jnp.logical_not(late)
    straight = (z >= nz // 2) & late

    loads = {}

    def load(name, source, target):
        copy = pltpu.make_async_copy(source, target, load_sem.at[len(loads)])
        copy.start()
        loads[name] = copy

    for s in reversed(range(sec_dev)):
        load(("wave", s), wave.at[pl.ds(s * width, width)], waves.at[s + 1])
    for i in range(sec_dev):
        s = jnp.where(mirrored, i, sec_dev - 1 - i)
        for p in range(pair_dev):
            load(("normal", i, p), left_normal.at[p, s], lefts.at[0, p, s])
        for p in range(pair_dev):
            load(("comp", i, p), left_comp.at[p, s], lefts.at[1, p, s])
        if i == 0:
            load("right_comp", right_comp, rights.at[0])
            load("right_normal", right_normal, rights.at[1])

    barrier = pltpu.get_barrier_semaphore()
    for d in range(1, nx):
        pl.semaphore_signal(barrier, inc=1, device_id=(z * nx + lax.rem(x + d, nx), sect), device_id_type=MESH)
    for d in range(1, nz):
        pl.semaphore_signal(barrier, inc=1, device_id=(lax.rem(z + d, nz) * nx + x, sect), device_id_type=MESH)
    for d in (1, ns - 1):
        pl.semaphore_signal(barrier, inc=1, device_id=(me, lax.rem(sect + d, ns)), device_id_type=MESH)

    def mask(s):
        loads[("wave", s)].wait()
        step = 64

        def body(i, _):
            at = pl.ds(i * step, step)
            row = lax.broadcasted_iota(jnp.int32, (step, 128), 0) + i * step
            keep = jnp.where(row < rows_ref[s], 1.0, 0.0).astype(BF16)
            for first in range(0, blocks * cols, 128):
                columns = slice(first, first + 128)
                waves[s + 1, at, columns] = waves[s + 1, at, columns] * keep
            return 0

        lax.fori_loop(0, width // step, body, 0)

    mask(sec_dev - 1)
    pl.semaphore_wait(barrier, nx - 1 + nz - 1 + 2)
    halo = pltpu.make_async_remote_copy(
        src_ref=waves.at[sec_dev],
        dst_ref=waves.at[0],
        send_sem=halo_send,
        recv_sem=halo_recv,
        device_id=(me, lax.rem(sect + 1, ns)),
        device_id_type=MESH,
    )

    @pl.when(sect < ns - 1)
    def _():
        halo.start()

    @pl.when(sect == 0)
    def _():
        waves[0] = jnp.zeros((width, blocks * cols), BF16)

    for s in reversed(range(sec_dev - 1)):
        mask(s)

    def order(k):
        down = nz - 1 - k
        at = jnp.where(mirrored, nz - 1 - z, z)
        c = jnp.where(k == nz - 1, at, jnp.where(down > at, down, down - 1))
        return jnp.where(mirrored, nz - 1 - c, c)

    def x_copy(c, d, j):
        return pltpu.make_async_remote_copy(
            src_ref=x_out.at[c, d - 1, j],
            dst_ref=x_in.at[c, d - 1, j],
            send_sem=x_send.at[c, d - 1, j],
            recv_sem=x_recv.at[c, d - 1, j],
            device_id=(z * nx + lax.rem(x + d, nx), sect),
            device_id_type=MESH,
        )

    def z_copy(c, j):
        return pltpu.make_async_remote_copy(
            src_ref=z_out.at[c, j],
            dst_ref=z_in.at[c, j],
            send_sem=z_send.at[c, j],
            recv_sem=z_recv.at[c, j],
            device_id=(partner * nx + x, sect),
            device_id_type=MESH,
        )

    def far_copy(c, j, slot):
        return pltpu.make_async_remote_copy(
            src_ref=z_out.at[c, j],
            dst_ref=far_in.at[slot, j],
            send_sem=z_send.at[c, j],
            recv_sem=far_recv.at[slot, j],
            device_id=(c * nx + x, sect),
            device_id_type=MESH,
        )

    def combines(c):
        above = (c // 2 > z // 2) & (lax.rem(z, 2) == 1)
        below = (c // 2 < z // 2) & (lax.rem(z, 2) == 0)
        return (above | below) & jnp.logical_not(straight)

    def wait_left(i, kind):
        for p in range(pair_dev):
            loads[(("normal", "comp")[kind], i, p)].wait()

    own_late = jnp.where(z >= nz // sec_dev, 1, 0)
    halo_step = jnp.where(mirrored, 0, nz - nz // sec_dev - own_late)

    def compute(k):
        c = order(k)
        s = c * chunk // width
        at = pl.ds(pl.multiple_of(c * chunk - s * width, chunk), chunk)
        for kind in range(2):

            @pl.when(k == 0)
            def _():
                wait_left(0, kind)

            @pl.when(k == nz // sec_dev - 1)
            def _():
                for i in range(1, sec_dev):
                    wait_left(i, kind)

            if kind == 1:

                @pl.when((k == halo_step) & (sect > 0))
                def _():
                    halo.wait_recv()

            for p in range(pair_dev):
                live = p < count_ref[0]
                offset = shift_ref[p]
                ops = lefts[kind, p, s, at, :]
                value = jnp.dot(ops, waves[s + 1 - kind], preferred_element_type=F32)
                value = jnp.where(live, value, 0.0).astype(BF16)
                pieces = [value[:, j * cols : (j + 1) * cols] for j in range(blocks)]
                for j in range(blocks):
                    piece = pieces[j]
                    for o in range(1, blocks):
                        piece = jnp.where(offset == o, pieces[(j + o) % blocks], piece)
                    applied[j, kind, p] = piece

        @pl.when(k == 0)
        def _():
            loads["right_comp"].wait()
            loads["right_normal"].wait()

        for j in range(blocks):
            result = None
            for kind in range(2):
                for p in range(pair_dev):
                    term = lax.dot_general(applied[j, kind, p], rights[kind, p, j], NT, preferred_element_type=F32)
                    result = term if result is None else result + term
            total[...] = result
            own[c, j] = total[pl.ds(pl.multiple_of(x * part, part), part), :]
            for d in range(1, nx):
                to = lax.rem(x + d, nx)
                x_out[c, d - 1, j] = total[pl.ds(pl.multiple_of(to * part, part), part), :].astype(BF16)
                x_copy(c, d, j).start()

    def x_sum(k):
        c = order(k)
        for j in range(blocks):
            value = own[c, j]
            for d in range(1, nx):
                x_copy(c, d, j).wait_recv()
                value = value + x_in[c, d - 1, j].astype(F32)
            own[c, j] = value

            @pl.when((c != z) & jnp.logical_not(combines(c)))
            def _():
                z_out[c, j] = value.astype(BF16)
                far = straight & (c // 2 != z // 2)

                @pl.when(far)
                def _():
                    far_copy(c, j, z).start()

                @pl.when(jnp.logical_not(far))
                def _():
                    z_copy(c, j).start()

    def z_sum(k):
        c = order(k)

        @pl.when((c != z) & combines(c))
        def _():
            for j in range(blocks):
                z_copy(c, j).wait_recv()
                z_out[c, j] = (own[c, j] + z_in[c, j].astype(F32)).astype(BF16)
                far_copy(c, j, z).start()

    def step(k, _):
        @pl.when(k < nz)
        def _():
            compute(k)

        @pl.when(k >= 2)
        def _():
            z_sum(k - 2)

        @pl.when((k >= 1) & (k <= nz))
        def _():
            x_sum(k - 1)

        return 0

    lax.fori_loop(0, nz + 1, step, 0)

    first = me * part
    row = lax.broadcasted_iota(jnp.int32, (part, cols), 0) + lax.rem(first, width)
    kept = row < rows_ref[first // width]
    for j in range(blocks):
        value = own[z, j]
        z_copy(z, j).wait_recv()
        value = value + z_in[z, j].astype(F32)
        for d in range(1, nz // 2):
            pair = lax.rem(z // 2 + d, nz // 2)
            inner = 2 * pair + jnp.where(pair < z // 2, 1, 0)
            far_copy(z, j, inner).wait_recv()
            value = value + far_in[inner, j].astype(F32)
        own[z, j] = value
        for d in range(1, nz // 2):
            pair = lax.rem(z // 2 + d, nz // 2)
            outer = 2 * pair + jnp.where(pair < z // 2, 0, 1)

            @pl.when(late & (2 * pair >= nz // 2))
            def _():
                far_copy(z, j, outer).wait_recv()
                own[z, j] = own[z, j] + far_in[outer, j].astype(F32)

        value = own[z, j]
        out_ref[:, j * cols : (j + 1) * cols] = jnp.where(kept, value, 0.0).astype(BF16)

    @pl.when(sect < ns - 1)
    def _():
        halo.wait_send()

    def drain(k, _):
        c = order(k)
        for j in range(blocks):
            for d in range(1, nx):
                x_copy(c, d, j).wait_send()

            @pl.when(c != z)
            def _():
                z_copy(c, j).wait_send()

        return 0

    lax.fori_loop(0, nz, drain, 0)


def solution(mesh):
    n_pairs, ns = mesh.shape["pairs"], mesh.shape["sect"]
    nx = x_size(n_pairs)
    nz = n_pairs // nx

    def local(wavefunction, left_normal, left_comp, right_comp, right_normal, pair_shift, pair_count, sector_rows):
        pair_dev, sec_dev, width, _ = left_normal.shape
        blocks, cols = right_comp.shape[1], right_comp.shape[2]
        chunk = sec_dev * width // nz
        part = chunk // nx
        dma = pltpu.SemaphoreType.DMA
        smem = pl.BlockSpec(memory_space=pltpu.SMEM)
        hbm = pl.BlockSpec(memory_space=pl.ANY)
        return pl.pallas_call(
            functools.partial(kernel, nz, nx, ns),
            out_shape=jax.ShapeDtypeStruct((part, blocks * cols), BF16),
            in_specs=[smem] * 3 + [hbm] * 5,
            out_specs=pl.BlockSpec(memory_space=pltpu.VMEM),
            scratch_shapes=[
                pltpu.VMEM((sec_dev + 1, width, blocks * cols), BF16),
                pltpu.VMEM((2, pair_dev, sec_dev, width, width), BF16),
                pltpu.VMEM((2, pair_dev, blocks, cols, cols), BF16),
                pltpu.VMEM((blocks, 2, pair_dev, chunk, cols), BF16),
                pltpu.VMEM((chunk, cols), F32),
                pltpu.VMEM((nz, blocks, part, cols), F32),
                pltpu.VMEM((nz, nx - 1, blocks, part, cols), BF16),
                pltpu.VMEM((nz, nx - 1, blocks, part, cols), BF16),
                pltpu.VMEM((nz, blocks, part, cols), BF16),
                pltpu.VMEM((nz, blocks, part, cols), BF16),
                pltpu.VMEM((nz, blocks, part, cols), BF16),
                dma((sec_dev + 2 * sec_dev * pair_dev + 2,)),
                dma,
                dma,
                dma((nz, nx - 1, blocks)),
                dma((nz, nx - 1, blocks)),
                dma((nz, blocks)),
                dma((nz, blocks)),
                dma((nz, blocks)),
            ],
            compiler_params=pltpu.CompilerParams(
                collective_id=0, has_side_effects=True, vmem_limit_bytes=62 * 2**20
            ),
        )(pair_shift, pair_count, sector_rows, wavefunction, left_normal, left_comp, right_comp, right_normal)

    placed = (
        P("sect", None),
        P("pairs", "sect", None, None),
        P("pairs", "sect", None, None),
        P("pairs", None, None, None),
        P("pairs", None, None, None),
        P("pairs"),
        P("pairs"),
        P("sect"),
    )
    return jax.shard_map(
        local, mesh=mesh, in_specs=placed, out_specs=P(("sect", "pairs"), None), check_vma=False
    )
```

```python
import functools

import jax
import jax.numpy as jnp
from jax import lax
from jax.experimental import pallas as pl
from jax.experimental.pallas import tpu as pltpu
from jax.sharding import PartitionSpec as P

MESH = pl.DeviceIdType.MESH
F32 = jnp.float32
BF16 = jnp.bfloat16
NT = (((1,), (1,)), ((), ()))


def x_size(count):
    return 1 << ((count.bit_length() - 1) // 2)


def kernel(
    nz,
    nx,
    ns,
    shift_ref,
    count_ref,
    rows_ref,
    wave,
    left_normal,
    left_comp,
    right_comp,
    right_normal,
    out_ref,
    waves,
    lefts,
    rights,
    applied,
    total,
    own,
    x_out,
    x_in,
    z_out,
    z_in,
    far_in,
    load_sem,
    halo_send,
    halo_recv,
    x_send,
    x_recv,
    z_send,
    z_recv,
    far_recv,
):
    pair_dev, sec_dev, width, _ = left_normal.shape
    blocks, cols = right_comp.shape[1], right_comp.shape[2]
    chunk = sec_dev * width // nz
    part = chunk // nx
    me = lax.axis_index("pairs")
    sect = lax.axis_index("sect")
    z = me // nx
    x = lax.rem(me, nx)
    partner = z + 1 - 2 * lax.rem(z, 2)

    late = (sect > 0) & (lax.rem(sect, 2) == 0)
    mirrored = (z >= nz // 2) & jnp.logical_not(late)
    straight = (z >= nz // 2) & late

    loads = {}

    def load(name, source, target):
        copy = pltpu.make_async_copy(source, target, load_sem.at[len(loads)])
        copy.start()
        loads[name] = copy

    for s in reversed(range(sec_dev)):
        load(("wave", s), wave.at[pl.ds(s * width, width)], waves.at[s + 1])
    for i in range(sec_dev):
        s = jnp.where(mirrored, i, sec_dev - 1 - i)
        for p in range(pair_dev):
            load(("normal", i, p), left_normal.at[p, s], lefts.at[0, p, s])
        for p in range(pair_dev):
            load(("comp", i, p), left_comp.at[p, s], lefts.at[1, p, s])
        if i == 0:
            load("right_comp", right_comp, rights.at[0])
            load("right_normal", right_normal, rights.at[1])

    barrier = pltpu.get_barrier_semaphore()
    for d in range(1, nx):
        pl.semaphore_signal(barrier, inc=1, device_id=(z * nx + lax.rem(x + d, nx), sect), device_id_type=MESH)
    for d in range(1, nz):
        pl.semaphore_signal(barrier, inc=1, device_id=(lax.rem(z + d, nz) * nx + x, sect), device_id_type=MESH)
    for d in (1, ns - 1):
        pl.semaphore_signal(barrier, inc=1, device_id=(me, lax.rem(sect + d, ns)), device_id_type=MESH)

    def mask(s):
        loads[("wave", s)].wait()
        step = 64

        def body(i, _):
            at = pl.ds(i * step, step)
            row = lax.broadcasted_iota(jnp.int32, (step, 128), 0) + i * step
            keep = jnp.where(row < rows_ref[s], 1.0, 0.0).astype(BF16)
            for first in range(0, blocks * cols, 128):
                columns = slice(first, first + 128)
                waves[s + 1, at, columns] = waves[s + 1, at, columns] * keep
            return 0

        lax.fori_loop(0, width // step, body, 0)

    mask(sec_dev - 1)
    pl.semaphore_wait(barrier, nx - 1 + nz - 1 + 2)
    halo = pltpu.make_async_remote_copy(
        src_ref=waves.at[sec_dev],
        dst_ref=waves.at[0],
        send_sem=halo_send,
        recv_sem=halo_recv,
        device_id=(me, lax.rem(sect + 1, ns)),
        device_id_type=MESH,
    )

    @pl.when(sect < ns - 1)
    def _():
        halo.start()

    @pl.when(sect == 0)
    def _():
        waves[0] = jnp.zeros((width, blocks * cols), BF16)

    for s in reversed(range(sec_dev - 1)):
        mask(s)

    def order(k):
        down = nz - 1 - k
        at = jnp.where(mirrored, nz - 1 - z, z)
        c = jnp.where(k == nz - 1, at, jnp.where(down > at, down, down - 1))
        return jnp.where(mirrored, nz - 1 - c, c)

    def x_copy(c, d, j):
        return pltpu.make_async_remote_copy(
            src_ref=x_out.at[c, d - 1, j],
            dst_ref=x_in.at[c, d - 1, j],
            send_sem=x_send.at[c, d - 1, j],
            recv_sem=x_recv.at[c, d - 1, j],
            device_id=(z * nx + lax.rem(x + d, nx), sect),
            device_id_type=MESH,
        )

    def z_copy(c, j):
        return pltpu.make_async_remote_copy(
            src_ref=z_out.at[c, j],
            dst_ref=z_in.at[c, j],
            send_sem=z_send.at[c, j],
            recv_sem=z_recv.at[c, j],
            device_id=(partner * nx + x, sect),
            device_id_type=MESH,
        )

    def far_copy(c, j, slot):
        return pltpu.make_async_remote_copy(
            src_ref=z_out.at[c, j],
            dst_ref=far_in.at[slot, j],
            send_sem=z_send.at[c, j],
            recv_sem=far_recv.at[slot, j],
            device_id=(c * nx + x, sect),
            device_id_type=MESH,
        )

    def combines(c):
        above = (c // 2 > z // 2) & (lax.rem(z, 2) == 1)
        below = (c // 2 < z // 2) & (lax.rem(z, 2) == 0)
        return (above | below) & jnp.logical_not(straight)

    def wait_left(i, kind):
        for p in range(pair_dev):
            loads[(("normal", "comp")[kind], i, p)].wait()

    own_late = jnp.where(z >= nz // sec_dev, 1, 0)
    halo_step = jnp.where(mirrored, 0, nz - nz // sec_dev - own_late)

    def compute(k):
        c = order(k)
        s = c * chunk // width
        at = pl.ds(pl.multiple_of(c * chunk - s * width, chunk), chunk)
        for kind in range(2):

            @pl.when(k == 0)
            def _():
                wait_left(0, kind)

            @pl.when(k == nz // sec_dev - 1)
            def _():
                for i in range(1, sec_dev):
                    wait_left(i, kind)

            if kind == 1:

                @pl.when((k == halo_step) & (sect > 0))
                def _():
                    halo.wait_recv()

            for p in range(pair_dev):
                live = p < count_ref[0]
                offset = shift_ref[p]
                ops = lefts[kind, p, s, at, :]
                value = jnp.dot(ops, waves[s + 1 - kind], preferred_element_type=F32)
                value = jnp.where(live, value, 0.0).astype(BF16)
                pieces = [value[:, j * cols : (j + 1) * cols] for j in range(blocks)]
                for j in range(blocks):
                    piece = pieces[j]
                    for o in range(1, blocks):
                        piece = jnp.where(offset == o, pieces[(j + o) % blocks], piece)
                    applied[j, kind, p] = piece

        @pl.when(k == 0)
        def _():
            loads["right_comp"].wait()
            loads["right_normal"].wait()

        for j in range(blocks):
            result = None
            for kind in range(2):
                for p in range(pair_dev):
                    term = lax.dot_general(applied[j, kind, p], rights[kind, p, j], NT, preferred_element_type=F32)
                    result = term if result is None else result + term
            total[...] = result
            own[c, j] = total[pl.ds(pl.multiple_of(x * part, part), part), :]
            for d in range(1, nx):
                to = lax.rem(x + d, nx)
                x_out[c, d - 1, j] = total[pl.ds(pl.multiple_of(to * part, part), part), :].astype(BF16)
                x_copy(c, d, j).start()

    def x_sum(k):
        c = order(k)
        for j in range(blocks):
            value = own[c, j]
            for d in range(1, nx):
                x_copy(c, d, j).wait_recv()
                value = value + x_in[c, d - 1, j].astype(F32)
            own[c, j] = value

            @pl.when((c != z) & jnp.logical_not(combines(c)))
            def _():
                z_out[c, j] = value.astype(BF16)
                far = straight & (c // 2 != z // 2)

                @pl.when(far)
                def _():
                    far_copy(c, j, z).start()

                @pl.when(jnp.logical_not(far))
                def _():
                    z_copy(c, j).start()

    def z_sum(k):
        c = order(k)

        @pl.when((c != z) & combines(c))
        def _():
            for j in range(blocks):
                z_copy(c, j).wait_recv()
                z_out[c, j] = (own[c, j] + z_in[c, j].astype(F32)).astype(BF16)
                far_copy(c, j, z).start()

    def step(k, _):
        early = straight & (k == nz - 1)

        @pl.when(early)
        def _():
            x_sum(k - 1)

        @pl.when(k < nz)
        def _():
            compute(k)

        @pl.when(k >= 2)
        def _():
            z_sum(k - 2)

        @pl.when((k >= 1) & (k <= nz) & jnp.logical_not(early))
        def _():
            x_sum(k - 1)

        return 0

    lax.fori_loop(0, nz + 1, step, 0)

    first = me * part
    row = lax.broadcasted_iota(jnp.int32, (part, cols), 0) + lax.rem(first, width)
    kept = row < rows_ref[first // width]
    for j in range(blocks):
        value = own[z, j]
        z_copy(z, j).wait_recv()
        value = value + z_in[z, j].astype(F32)
        for d in range(1, nz // 2):
            pair = lax.rem(z // 2 + d, nz // 2)
            inner = 2 * pair + jnp.where(pair < z // 2, 1, 0)
            far_copy(z, j, inner).wait_recv()
            value = value + far_in[inner, j].astype(F32)
        own[z, j] = value
        for d in range(1, nz // 2):
            pair = lax.rem(z // 2 + d, nz // 2)
            outer = 2 * pair + jnp.where(pair < z // 2, 0, 1)

            @pl.when(late & (2 * pair >= nz // 2))
            def _():
                far_copy(z, j, outer).wait_recv()
                own[z, j] = own[z, j] + far_in[outer, j].astype(F32)

        value = own[z, j]
        out_ref[:, j * cols : (j + 1) * cols] = jnp.where(kept, value, 0.0).astype(BF16)

    @pl.when(sect < ns - 1)
    def _():
        halo.wait_send()

    def drain(k, _):
        c = order(k)
        for j in range(blocks):
            for d in range(1, nx):
                x_copy(c, d, j).wait_send()

            @pl.when(c != z)
            def _():
                z_copy(c, j).wait_send()

        return 0

    lax.fori_loop(0, nz, drain, 0)


def solution(mesh):
    n_pairs, ns = mesh.shape["pairs"], mesh.shape["sect"]
    nx = x_size(n_pairs)
    nz = n_pairs // nx

    def local(wavefunction, left_normal, left_comp, right_comp, right_normal, pair_shift, pair_count, sector_rows):
        pair_dev, sec_dev, width, _ = left_normal.shape
        blocks, cols = right_comp.shape[1], right_comp.shape[2]
        chunk = sec_dev * width // nz
        part = chunk // nx
        dma = pltpu.SemaphoreType.DMA
        smem = pl.BlockSpec(memory_space=pltpu.SMEM)
        hbm = pl.BlockSpec(memory_space=pl.ANY)
        return pl.pallas_call(
            functools.partial(kernel, nz, nx, ns),
            out_shape=jax.ShapeDtypeStruct((part, blocks * cols), BF16),
            in_specs=[smem] * 3 + [hbm] * 5,
            out_specs=pl.BlockSpec(memory_space=pltpu.VMEM),
            scratch_shapes=[
                pltpu.VMEM((sec_dev + 1, width, blocks * cols), BF16),
                pltpu.VMEM((2, pair_dev, sec_dev, width, width), BF16),
                pltpu.VMEM((2, pair_dev, blocks, cols, cols), BF16),
                pltpu.VMEM((blocks, 2, pair_dev, chunk, cols), BF16),
                pltpu.VMEM((chunk, cols), F32),
                pltpu.VMEM((nz, blocks, part, cols), F32),
                pltpu.VMEM((nz, nx - 1, blocks, part, cols), BF16),
                pltpu.VMEM((nz, nx - 1, blocks, part, cols), BF16),
                pltpu.VMEM((nz, blocks, part, cols), BF16),
                pltpu.VMEM((nz, blocks, part, cols), BF16),
                pltpu.VMEM((nz, blocks, part, cols), BF16),
                dma((sec_dev + 2 * sec_dev * pair_dev + 2,)),
                dma,
                dma,
                dma((nz, nx - 1, blocks)),
                dma((nz, nx - 1, blocks)),
                dma((nz, blocks)),
                dma((nz, blocks)),
                dma((nz, blocks)),
            ],
            compiler_params=pltpu.CompilerParams(
                collective_id=0, has_side_effects=True, vmem_limit_bytes=62 * 2**20
            ),
        )(pair_shift, pair_count, sector_rows, wavefunction, left_normal, left_comp, right_comp, right_normal)

    placed = (
        P("sect", None),
        P("pairs", "sect", None, None),
        P("pairs", "sect", None, None),
        P("pairs", None, None, None),
        P("pairs", None, None, None),
        P("pairs"),
        P("pairs"),
        P("sect"),
    )
    return jax.shard_map(
        local, mesh=mesh, in_specs=placed, out_specs=P(("sect", "pairs"), None), check_vma=False
    )
```
